256 devices in a mesh: gx: 16 (over x, z_hi, core), gy: 4 (over z_lo), gz: 4 (over y).
Axes of the slice: x: 4, y: 4, z: 8 (z_hi: 2, z_lo: 4; z = z_hi * 4 + z_lo), core: 2. Of those that a mesh axis runs over, the one named last changes fastest.
Arguments:
- position: float32 [3, 16, 4, 4, 4096], P(None, 'gx', 'gy', 'gz'), may hold values from 0 to 4
- velocity: float32 [3, 16, 4, 4, 4096], P(None, 'gx', 'gy', 'gz'), may hold values from -4 to 4
- radius: float32 [16, 4, 4, 4096], P('gx', 'gy', 'gz'), may hold values from 0.5 to 1
- vertices: float32 [9, 16, 4, 4, 2048], P(None, 'gx', 'gy', 'gz'), may hold values from 0 to 4
- vertex_speed: float32 [9, 16, 4, 4, 2048], P(None, 'gx', 'gy', 'gz'), may hold values from -4 to 4
- angles: float32 [3], replicated, may hold values from 0.1 to 0.4
- ghost_blocks: int32 [16, 4, 4, 16], P('gx', 'gy', 'gz'), may hold values from 0 to 31
- tile_home: int32 [16, 4, 4, 64], P('gx', 'gy', 'gz'), may hold values from 0 to 31
- tile_other: int32 [16, 4, 4, 64], P('gx', 'gy', 'gz'), may hold values from 0 to 127
- wall_home: int32 [16, 4, 4, 32], P('gx', 'gy', 'gz'), may hold values from 0 to 31
- wall_block: int32 [16, 4, 4, 32], P('gx', 'gy', 'gz'), may hold values from 0 to 255
- mig_order: int32 [3, 16, 4, 4, 4096], P(None, 'gx', 'gy', 'gz'), may hold values from 0 to 4095, each once within a row
- mig_count: int32 [3, 16, 4, 4, 16], P(None, 'gx', 'gy', 'gz'), may hold values from 0 to 16, as said below
Outputs:
- position_out: float32 [3, 16, 4, 4, 4096], P(None, 'gx', 'gy', 'gz')
- velocity_out: float32 [3, 16, 4, 4, 4096], P(None, 'gx', 'gy', 'gz')
- radius_out: float32 [16, 4, 4, 4096], P('gx', 'gy', 'gz')
The draws below stay inside these ranges and needn't reach their ends.
Inputs may be any that keep to these rules, and one draw needn't show every extreme that they name: Within every step and slab, mig_count of device p for peer q equals that of q for p, is 0 for p itself, and is 16 for the first two devices of the slab toward each other.
All inputs are finite; a program needn't handle non-finite values.
Results may differ from the reference program's by a relative error of at most 0.0003.
Values sent between devices are 32-bit elements; how exact they have to be, the bound alone decides.
A program may use at most 64 MiB of HBM per device.

```python
import jax
import jax.numpy as jnp
from jax import lax

PART_DEV = 4096
TRI_DEV = 2048
GHOST = 16
TILES = 64
TTILES = 32
MC = 16
STEPS = 3
NBLK = 32
POOL = 128
SLABS = 16
CYCLES = 4
SECTORS = 4
GROUP = 16
COLTRI = 256


def draw_mig_count(key, part):
    key = jax.random.fold_in(key, 7)
    raw_counts = jax.random.randint(key, (STEPS, SLABS, GROUP, GROUP), 0, MC + 1)
    paired = jnp.maximum(raw_counts, jnp.swapaxes(raw_counts, 2, 3))
    paired = paired * (1 - jnp.eye(GROUP, dtype=jnp.int32))
    paired = paired.at[:, :, 0, 1].set(MC).at[:, :, 1, 0].set(MC)
    return paired.reshape(STEPS, SLABS, CYCLES, SECTORS, GROUP).astype(jnp.int32)


def plant(entries, own_key, least, high):
    extent = entries.shape
    spot = [jax.random.randint(jax.random.fold_in(own_key, axis), (), 0, extent[axis]) for axis in range(len(extent))]
    entries = entries.at[tuple(spot)].set(least)
    longest = extent.index(max(extent))
    spot[longest] = (spot[longest] + 1) % extent[longest]
    return entries.at[tuple(spot)].set(high)


def level_of(rng, shape, shards, smallest, top_value):
    factor_of, own = 1.0, jax.random.fold_in(rng, 6)
    for dim, blocks in shards:
        draws = jnp.exp(jax.random.uniform(jax.random.fold_in(own, dim), (blocks,), jnp.float32, smallest / len(shards), top_value / len(shards)))
        factor_of = factor_of * jnp.repeat(draws, shape[dim] // blocks).reshape([-1 if axis == dim else 1 for axis in range(len(shape))])
    return factor_of


def scatter_about(stream_key, dims, scale, most, cuts=(), kind=jnp.bfloat16):
    factor_of = level_of(stream_key, dims, cuts, -0.22, 0.18) if cuts else 1.0
    values = jax.random.normal(stream_key, dims, jnp.float32) * scale * factor_of
    return jnp.minimum(jnp.maximum(values, -most), most).astype(kind)


def setup_inputs(seed: int = 0) -> dict:
    key_list = jax.random.split(jax.random.key(seed), 14)
    position = jnp.clip(4.0 * jax.random.uniform(key_list[0], (3, SLABS, CYCLES, SECTORS, PART_DEV), jnp.float32) ** level_of(key_list[0], (3, SLABS, CYCLES, SECTORS, PART_DEV), ((1, 16), (2, 4), (3, 4)), -0.2, 0.2), 0.0, 4.0)
    velocity = scatter_about(key_list[1], (3, SLABS, CYCLES, SECTORS, PART_DEV), 1.0, 4.0, ((1, 16), (2, 4), (3, 4)), jnp.float32)
    radius = jnp.clip(0.5 + 0.5 * jax.random.uniform(key_list[2], (SLABS, CYCLES, SECTORS, PART_DEV), jnp.float32) ** level_of(key_list[2], (SLABS, CYCLES, SECTORS, PART_DEV), ((0, 16), (1, 4), (2, 4)), -0.2, 0.2), 0.5, 1.0)
    vertices = jnp.clip(4.0 * jax.random.uniform(key_list[3], (9, SLABS, CYCLES, SECTORS, TRI_DEV), jnp.float32) ** level_of(key_list[3], (9, SLABS, CYCLES, SECTORS, TRI_DEV), ((1, 16), (2, 4), (3, 4)), -0.2, 0.2), 0.0, 4.0)
    vertex_speed = scatter_about(key_list[4], (9, SLABS, CYCLES, SECTORS, TRI_DEV), 1.0, 4.0, ((1, 16), (2, 4), (3, 4)), jnp.float32)
    angles = jnp.clip(jax.random.uniform(key_list[5], (STEPS,), jnp.float32, 0.1, 0.4), 0.1, 0.4)
    ghost_blocks = plant(jax.random.randint(key_list[6], (SLABS, CYCLES, SECTORS, GHOST), 0, NBLK), jax.random.fold_in(key_list[6], 1), 0, NBLK - 1).astype(jnp.int32)
    tile_home = plant(jax.random.randint(key_list[7], (SLABS, CYCLES, SECTORS, TILES), 0, NBLK), jax.random.fold_in(key_list[7], 1), 0, NBLK - 1).astype(jnp.int32)
    tile_other = plant(jax.random.randint(key_list[8], (SLABS, CYCLES, SECTORS, TILES), 0, POOL), jax.random.fold_in(key_list[8], 1), 0, POOL - 1).astype(jnp.int32)
    wall_home = plant(jax.random.randint(key_list[9], (SLABS, CYCLES, SECTORS, TTILES), 0, NBLK), jax.random.fold_in(key_list[9], 1), 0, NBLK - 1).astype(jnp.int32)
    wall_block = plant(jax.random.randint(key_list[10], (SLABS, CYCLES, SECTORS, TTILES), 0, COLTRI), jax.random.fold_in(key_list[10], 1), 0, COLTRI - 1).astype(jnp.int32)
    mig_order = jax.vmap(lambda own: jax.random.permutation(own, PART_DEV))(jax.random.split(key_list[11], STEPS * SLABS * CYCLES * SECTORS)).reshape((STEPS, SLABS, CYCLES, SECTORS, PART_DEV)).astype(jnp.int32)
    mig_count = draw_mig_count(jax.random.fold_in(key_list[13], 71), 0)
    return dict(position=position, velocity=velocity, radius=radius, vertices=vertices, vertex_speed=vertex_speed, angles=angles, ghost_blocks=ghost_blocks, tile_home=tile_home, tile_other=tile_other, wall_home=wall_home, wall_block=wall_block, mig_order=mig_order, mig_count=mig_count)


STIFFNESS = 20.0
DAMPING = 2.0
WALL_STIFF = 20.0
SOFTENING = 0.01
TIME_STEP = 0.02
GRAVITY = 1.0
AXIS_CENTRE = 2.0
AREA_FLOOR = 1.0
SPREAD_PAD = 0.25

def blade_move(corners, speeds, angle_now):
    cosine = jnp.cos(angle_now)
    sine_val = jnp.sin(angle_now)
    row_list = []
    for corner in range(3):
        along_x = corners[3 * corner]
        rel_y = corners[3 * corner + 1] - AXIS_CENTRE
        rel_z = corners[3 * corner + 2] - AXIS_CENTRE
        row_list += [along_x, AXIS_CENTRE + cosine * rel_y - sine_val * rel_z, AXIS_CENTRE + sine_val * rel_y + cosine * rel_z]
    return jnp.stack(row_list) + TIME_STEP * speeds

def pair_force(home_rows, other_rows):
    offset = home_rows[0:3, :, None] - other_rows[0:3, None, :]
    distance = jnp.sqrt(lax.optimization_barrier(jnp.sum(offset * offset, axis=0)) + SOFTENING)
    relative = home_rows[3:6, :, None] - other_rows[3:6, None, :]
    approach = lax.optimization_barrier(jnp.sum(relative * offset, axis=0)) / distance
    home_radius = home_rows[6][:, None]
    other_radius = other_rows[6][None, :]
    intersection = jnp.maximum(home_radius + other_radius - distance, 0.0)
    reduced = home_radius * other_radius / (home_radius + other_radius)
    magnitude = reduced * intersection * (STIFFNESS - DAMPING * approach) / distance
    return lax.optimization_barrier(jnp.sum(magnitude[None] * offset, axis=2))

def wall_force(home_rows, triangles):
    corner_a = triangles[0:3]
    corner_b = triangles[3:6]
    corner_c = triangles[6:9]
    centre = (corner_a + corner_b + corner_c) / 3.0
    area_vector = jnp.cross(corner_b - corner_a, corner_c - corner_a, axis=0)
    length = jnp.sqrt(lax.optimization_barrier(jnp.sum(area_vector * area_vector, axis=0)))
    normal = area_vector / jnp.maximum(length, AREA_FLOOR)
    spread = (lax.optimization_barrier(jnp.sum((corner_a - centre) ** 2, axis=0)) + lax.optimization_barrier(jnp.sum((corner_b - centre) ** 2, axis=0)) + lax.optimization_barrier(jnp.sum((corner_c - centre) ** 2, axis=0))) / 3.0 + SPREAD_PAD
    offset = home_rows[0:3, :, None] - centre[:, None, :]
    height = lax.optimization_barrier(jnp.sum(normal[:, None, :] * offset, axis=0))
    window = jnp.maximum(1.0 - lax.optimization_barrier(jnp.sum(offset * offset, axis=0)) / spread[None, :], 0.0)
    home_radius = home_rows[6][:, None]
    strength = WALL_STIFF * home_radius * jnp.maximum(home_radius - jnp.abs(height), 0.0) * height * window
    return lax.optimization_barrier(jnp.sum(strength[None] * normal[:, None, :], axis=2))

def shifted(blocks, axis_id, from_lower):
    widths = [(0, 0)] * blocks.ndim
    if from_lower:
        widths[axis_id] = (1, 0)
        padded = jnp.pad(blocks, widths)
        return lax.slice_in_dim(padded, 0, blocks.shape[axis_id], axis=axis_id)
    widths[axis_id] = (0, 1)
    padded = jnp.pad(blocks, widths)
    return lax.slice_in_dim(padded, 1, blocks.shape[axis_id] + 1, axis=axis_id)

def place_rows(rows_now, slot_ids, values):
    return rows_now.at[:, slot_ids].set(values)

def migrate(bodies, order_now, count_now):
    grouped = bodies.reshape(7, SLABS, GROUP, PART_DEV)
    slot_ids = order_now.reshape(SLABS, GROUP, PART_DEV)[:, :, :GROUP * MC]
    picks = jnp.broadcast_to(slot_ids[None], (7, SLABS, GROUP, GROUP * MC))
    outgoing = jnp.take_along_axis(grouped, picks, axis=3).reshape(7, SLABS, GROUP, GROUP, MC)
    arrived = jnp.swapaxes(outgoing, 2, 3)
    filled = jnp.arange(MC, dtype=jnp.int32)[None, None, None, :] < count_now.reshape(SLABS, GROUP, GROUP)[..., None]
    merged = jnp.where(filled[None], arrived, outgoing).reshape(7, SLABS, GROUP, GROUP * MC)
    inner = jax.vmap(place_rows, in_axes=(1, 0, 1), out_axes=1)
    outer = jax.vmap(inner, in_axes=(1, 0, 1), out_axes=1)
    return outer(grouped, slot_ids, merged).reshape(bodies.shape)

def reference(position, velocity, radius, vertices, vertex_speed, angles, ghost_blocks, tile_home, tile_other, wall_home, wall_block, mig_order, mig_count):
    device_total = SLABS * CYCLES * SECTORS
    bodies = jnp.concatenate([position, velocity, radius[None]], axis=0)
    corners = vertices
    home_all = tile_home.reshape(device_total, TILES)
    other_all = tile_other.reshape(device_total, TILES)
    wall_all = wall_home.reshape(device_total, TTILES)
    wblock_all = wall_block.reshape(device_total, TTILES)
    for sweep in range(STEPS):
        corners = blade_move(corners, vertex_speed, angles[sweep])
        columns = jnp.transpose(corners, (2, 3, 0, 1, 4)).reshape(CYCLES, SECTORS, 9, COLTRI, 128)
        blocks_all = bodies.reshape(7, SLABS, CYCLES, SECTORS, NBLK, 128)
        picks = jnp.broadcast_to(ghost_blocks[None, :, :, :, :, None], (7, SLABS, CYCLES, SECTORS, GHOST, 128))
        lent = jnp.take_along_axis(blocks_all, picks, axis=4)
        face_list = [shifted(lent, 1, True), shifted(lent, 1, False), shifted(lent, 2, True), shifted(lent, 2, False), shifted(lent, 3, True), shifted(lent, 3, False)]
        ghost_pool = jnp.concatenate([blocks_all] + face_list, axis=4)
        pool_dev = jnp.transpose(ghost_pool, (1, 2, 3, 0, 4, 5)).reshape(device_total, 7, POOL, 128)

        def one_device(packed):
            device_idx, pool_rows, home_ids, other_ids, wall_ids, wall_picks = packed
            cycle_idx = device_idx // SECTORS % CYCLES
            sector_idx = device_idx % SECTORS
            column = columns[cycle_idx, sector_idx]
            own_rows = pool_rows[:, :NBLK]
            pair_terms = jax.vmap(pair_force, in_axes=(1, 1))(own_rows[:, home_ids], pool_rows[:, other_ids])
            wall_terms = jax.vmap(wall_force, in_axes=(1, 1))(own_rows[:, wall_ids], column[:, wall_picks])
            summed = jnp.zeros((NBLK, 3, 128), jnp.float32).at[home_ids].add(pair_terms).at[wall_ids].add(wall_terms)
            return jnp.transpose(summed, (1, 0, 2)).reshape(3, PART_DEV)
        forces = lax.map(one_device, (jnp.arange(device_total, dtype=jnp.int32), pool_dev, home_all, other_all, wall_all, wblock_all))
        forces = jnp.transpose(forces.reshape(SLABS, CYCLES, SECTORS, 3, PART_DEV), (3, 0, 1, 2, 4))
        inertia = bodies[6] * bodies[6] * bodies[6]
        gravity_vec = jnp.array([0.0, 0.0, -GRAVITY], jnp.float32).reshape(3, 1, 1, 1, 1)
        new_velocity = bodies[3:6] + TIME_STEP * (forces / inertia[None] + gravity_vec)
        new_position = bodies[0:3] + TIME_STEP * new_velocity
        bodies = jnp.concatenate([new_position, new_velocity, bodies[6:7]], axis=0)
        bodies = migrate(bodies, mig_order[sweep], mig_count[sweep])
    return (bodies[0:3], bodies[3:6], bodies[6])
```

```python
import functools

import jax
import jax.numpy as jnp
from jax import lax
from jax.experimental import pallas as pl
from jax.experimental.pallas import tpu as pltpu
from jax.sharding import PartitionSpec as P

MESH = pl.DeviceIdType.MESH
F32 = jnp.float32
BF16 = jnp.bfloat16

STEPS = 3
NBLK = 32
GHOST = 16
POOL = 128
TILES = 64
TTILES = 32
TRIBLK = 16
SLABS = 16
GROUP = 16
MC = 16

STIFFNESS = 20.0
DAMPING = 2.0
WALL_STIFF = 20.0
SOFTENING = 0.01
TIME_STEP = 0.02
GRAVITY = 1.0
AXIS_CENTRE = 2.0
AREA_FLOOR = 1.0
SPREAD_PAD = 0.25


def split3(values):
    high = values.astype(BF16)
    rest = values - high.astype(F32)
    middle = rest.astype(BF16)
    low = (rest - middle.astype(F32)).astype(BF16)
    return high, middle, low


def split2(values):
    high = values.astype(BF16)
    low = (values - high.astype(F32)).astype(BF16)
    return high, low


def rows_of(block):
    return [block[i : i + 1, :] for i in range(8)]


def kernel(
    pos_h, vel_h, rad_h, vert_h, speed_h, order_h, angles, ghost_ids, home_ids, other_ids,
    wall_ids, wall_picks, counts,
    pos_o, vel_o, rad_o,
    bodies, corners, speeds, order, own, pool_0, pool_1, pool_2, lent, tri_0, tri_1, tri_2,
    outgoing, arrived, lane_hot, block_hot,
    pair_sel, wall_sel, pair_out, wall_out,
    in_sem, ghost_send, ghost_recv, mig_send, mig_recv,
    zh_send, zh_recv, x_send, x_recv, xz_send, xz_recv, core_send, core_recv,
):
    pool, tri = (pool_0, pool_1, pool_2), (tri_0, tri_1, tri_2)
    gx = lax.axis_index("gx")
    gy = lax.axis_index("gy")
    gz = lax.axis_index("gz")
    me = gy * 4 + gz
    x_at, zh, core = gx // 4, (gx // 2) % 2, gx % 2
    twin = gx + 1 - 2 * core
    zmate = gx + 2 - 4 * zh

    loads = [
        pltpu.make_async_copy(vert_h, corners, in_sem.at[0]),
        pltpu.make_async_copy(speed_h, speeds, in_sem.at[1]),
        pltpu.make_async_copy(pos_h, bodies.at[pl.ds(0, 3)], in_sem.at[2]),
        pltpu.make_async_copy(vel_h, bodies.at[pl.ds(3, 3)], in_sem.at[3]),
        pltpu.make_async_copy(rad_h, bodies.at[6], in_sem.at[4]),
        pltpu.make_async_copy(order_h.at[:, pl.ds(0, 8), :], order, in_sem.at[5]),
    ]
    for load in loads:
        load.start()

    def peer_of(hop):
        peer = lax.rem(me + hop, GROUP)
        return peer, (gx, peer // 4, peer % 4)

    def x_mate(hop, z_of):
        index = lax.rem(x_at + hop, 4) * 4 + z_of * 2 + core
        return index

    faces = [
        (gx > 0, gx < SLABS - 1, (gx + 1, gy, gz)),
        (gx < SLABS - 1, gx > 0, (gx - 1, gy, gz)),
        (gy > 0, gy < 3, (gx, gy + 1, gz)),
        (gy < 3, gy > 0, (gx, gy - 1, gz)),
        (gz > 0, gz < 3, (gx, gy, gz + 1)),
        (gz < 3, gz > 0, (gx, gy, gz - 1)),
    ]

    barrier = pltpu.get_barrier_semaphore()

    def greet(hop, carry):
        pl.semaphore_signal(barrier, inc=1, device_id=peer_of(hop)[1], device_id_type=MESH)
        return carry

    lax.fori_loop(1, GROUP, greet, 0)
    for other in (twin, zmate, x_mate(1, zh), x_mate(2, zh), x_mate(3, zh)):
        pl.semaphore_signal(barrier, inc=1, device_id=(other, gy, gz), device_id_type=MESH)
    for _, borrower, target in faces[:2]:
        @pl.when(borrower)
        def _():
            pl.semaphore_signal(barrier, inc=1, device_id=target, device_id_type=MESH)

    def ghost_copy(step, face, target):
        return pltpu.make_async_remote_copy(
            src_ref=lent.at[step],
            dst_ref=pool[step].at[pl.ds(NBLK + GHOST * face, GHOST)],
            send_sem=ghost_send.at[step, face],
            recv_sem=ghost_recv.at[step, face],
            device_id=target,
            device_id_type=MESH,
        )

    def tri_copy(step, owner, target, send, recv):
        part = tri[step].at[pl.ds(owner * TRIBLK, TRIBLK)]
        return pltpu.make_async_remote_copy(
            src_ref=part,
            dst_ref=part,
            send_sem=send,
            recv_sem=recv,
            device_id=(target, gy, gz),
            device_id_type=MESH,
        )

    def zh_copy(step):
        return tri_copy(step, gx, zmate, zh_send.at[step], zh_recv.at[step])

    def core_copy(step, owner, slot):
        return tri_copy(step, owner, twin, core_send.at[step, slot], core_recv.at[step, slot])

    def x_copy(step, hop):
        return tri_copy(step, gx, x_mate(hop, zh), x_send.at[step, hop - 1], x_recv.at[step, hop - 1])

    def xz_copy(step, hop):
        return tri_copy(step, zmate, x_mate(hop, zh), xz_send.at[step, hop - 1], xz_recv.at[step, hop - 1])

    def mig_copy(step, hop):
        peer, target = peer_of(hop)
        return pltpu.make_async_remote_copy(
            src_ref=outgoing.at[step, peer // 8],
            dst_ref=arrived.at[step, me],
            send_sem=mig_send.at[step, hop],
            recv_sem=mig_recv.at[step, hop],
            device_id=target,
            device_id_type=MESH,
        )

    def send_ghosts(step):
        for row in range(7):
            own[:, row, :] = bodies[row]
        own[:, 7, :] = jnp.zeros((NBLK, 128), F32)
        for slot in range(GHOST):
            lent[step, slot] = own[ghost_ids[slot]]
        for face, (_, borrower, target) in enumerate(faces):
            @pl.when(borrower)
            def _():
                ghost_copy(step, face, target).start()
        pool[step][pl.ds(0, NBLK)] = own[...]

    def wait_ghosts(step):
        for face, (lender, _, target) in enumerate(faces):
            @pl.when(lender)
            def _():
                ghost_copy(step, face, target).wait_recv()

    def blade_move(step):
        angle = jnp.full((8, 128), angles[step], F32)
        cosine = jnp.cos(angle)[0:1]
        sine = jnp.sin(angle)[0:1]
        now = []
        for corner in range(3):
            along = corners[3 * corner]
            rel_y = corners[3 * corner + 1] - AXIS_CENTRE
            rel_z = corners[3 * corner + 2] - AXIS_CENTRE
            for j, value in enumerate((
                along,
                AXIS_CENTRE + cosine * rel_y - sine * rel_z,
                AXIS_CENTRE + sine * rel_y + cosine * rel_z,
            )):
                moved = value + TIME_STEP * speeds[3 * corner + j]
                corners[3 * corner + j] = moved
                now.append(moved)
        a, b, c = now[0:3], now[3:6], now[6:9]
        centre = [(a[i] + b[i] + c[i]) / 3.0 for i in range(3)]
        u = [b[i] - a[i] for i in range(3)]
        w = [c[i] - a[i] for i in range(3)]
        area = [
            u[1] * w[2] - u[2] * w[1],
            u[2] * w[0] - u[0] * w[2],
            u[0] * w[1] - u[1] * w[0],
        ]
        length = jnp.sqrt(area[0] * area[0] + area[1] * area[1] + area[2] * area[2])
        scale = 1.0 / jnp.maximum(length, AREA_FLOOR)
        normal = [area[i] * scale for i in range(3)]
        spread = SPREAD_PAD
        for corner in (a, b, c):
            for i in range(3):
                spread = spread + (corner[i] - centre[i]) ** 2 * (1.0 / 3.0)
        level = normal[0] * centre[0] + normal[1] * centre[1] + normal[2] * centre[2]
        rows = normal + centre + [1.0 / spread, level]
        for row in range(8):
            tri[step][pl.ds(gx * TRIBLK, TRIBLK), row, :] = rows[row]

    def start_tri(step):
        blade_move(step)
        zh_copy(step).start()
        core_copy(step, gx, 0).start()
        for hop in (1, 2, 3):
            x_copy(step, hop).start()

    def forward_tri(step):
        zh_copy(step).wait_recv()
        for hop in (1, 2, 3):
            xz_copy(step, hop).start()
        core_copy(step, zmate, 1).start()

    def finish_tri(step):
        for hop in (1, 2, 3):
            x_copy(step, hop).wait_recv()
            core_copy(step, x_mate(4 - hop, zh), 1 + hop).start()
        for hop in (1, 2, 3):
            xz_copy(step, hop).wait_recv()
            core_copy(step, x_mate(4 - hop, 1 - zh), 4 + hop).start()

    def wait_tri(step):
        for slot in range(8):
            core_copy(step, gx, slot).wait_recv()

    def prepare():
        lane = lax.broadcasted_iota(jnp.int32, (128, 256), 0)
        block = lax.broadcasted_iota(jnp.int32, (NBLK, 256), 0)
        place = lax.broadcasted_iota(jnp.int32, (1, 256), 1)
        for step in range(STEPS):
            ids = jnp.concatenate([order[step, 0:1, :], order[step, 1:2, :]], axis=1)
            lane_hot[step] = (jnp.bitwise_and(ids, 127) == lane).astype(F32).astype(BF16)
            limit = jnp.zeros((1, 256), jnp.int32)
            for peer in range(GROUP):
                limit = jnp.where(lax.shift_right_logical(place, 4) == peer, counts[step, peer], limit)
            filled = jnp.bitwise_and(place, 15) < limit
            hot = lax.shift_right_logical(ids, 7) == block
            block_hot[step, 0] = hot.astype(F32)
            block_hot[step, 1] = jnp.logical_and(hot, filled).astype(F32)
        home = lax.broadcasted_iota(jnp.int32, (1, 128), 1)
        for tile in range(TILES):
            pair_sel[pl.ds(tile, 1)] = (home == home_ids[tile]).astype(F32)
        for tile in range(TTILES):
            wall_sel[pl.ds(tile, 1)] = (home == wall_ids[tile]).astype(F32)

    def pair_forces(step):
        def tile_body(tile, carry):
            mine = rows_of(own[home_ids[tile]])
            px, py, pz, pu, pv, pw, pr, _ = [jnp.broadcast_to(r, (8, 128)) for r in mine]
            theirs = pool[step][other_ids[tile]].T
            force = [jnp.zeros((8, 128), F32) for _ in range(3)]
            for part in range(16):
                q = theirs[8 * part : 8 * part + 8, :]
                qx, qy, qz, qu, qv, qw, qr = [
                    jnp.broadcast_to(q[:, i : i + 1], (8, 128)) for i in range(7)
                ]
                dx, dy, dz = px - qx, py - qy, pz - qz
                square = dx * dx + dy * dy + dz * dz + SOFTENING
                speed = (pu - qu) * dx + (pv - qv) * dy + (pw - qw) * dz
                reach = pr + qr
                scaled = square * reach
                ratio = lax.rsqrt(scaled * reach)
                dist = scaled * ratio
                over = reach * ratio
                overlap = jnp.maximum(reach - dist, 0.0)
                factor = STIFFNESS - (DAMPING * speed) * over
                strength = qr * ratio * overlap * factor
                force[0] += strength * dx
                force[1] += strength * dy
                force[2] += strength * dz
            for i in range(3):
                total = jnp.sum(force[i], axis=0, keepdims=True) * mine[6]
                pair_out[i, pl.ds(tile, 1)] = total
            return carry

        lax.fori_loop(0, TILES, tile_body, 0)

    def wall_forces(step):
        def tile_body(tile, carry):
            mine = rows_of(own[wall_ids[tile]])
            px, py, pz = [jnp.broadcast_to(r, (8, 128)) for r in mine[0:3]]
            pr = jnp.broadcast_to(mine[6], (8, 128))
            blades = tri[step][wall_picks[tile]].T
            force = [jnp.zeros((8, 128), F32) for _ in range(3)]
            for part in range(16):
                q = blades[8 * part : 8 * part + 8, :]
                nx, ny, nz, cx, cy, cz, narrow, level = [
                    jnp.broadcast_to(q[:, i : i + 1], (8, 128)) for i in range(8)
                ]
                dx, dy, dz = px - cx, py - cy, pz - cz
                height = nx * dx + ny * dy + nz * dz
                window = jnp.maximum(1.0 - (dx * dx + dy * dy + dz * dz) * narrow, 0.0)
                strength = jnp.maximum(pr - jnp.abs(height), 0.0) * height * window
                force[0] += strength * nx
                force[1] += strength * ny
                force[2] += strength * nz
            for i in range(3):
                total = jnp.sum(force[i], axis=0, keepdims=True) * (WALL_STIFF * mine[6])
                wall_out[i, pl.ds(tile, 1)] = total
            return carry

        lax.fori_loop(0, TTILES, tile_body, 0)

    def integrate():
        select = jnp.concatenate([pair_sel[...], wall_sel[...]], axis=0).T[0:NBLK].astype(BF16)
        radius = bodies[6]
        inertia = 1.0 / (radius * radius * radius)
        for i in range(3):
            high, low = split2(jnp.concatenate([pair_out[i], wall_out[i]], axis=0))
            force = jnp.dot(select, high, preferred_element_type=F32)
            force = force + jnp.dot(select, low, preferred_element_type=F32)
            pull = force * inertia
            if i == 2:
                pull = pull - GRAVITY
            velocity = bodies[3 + i] + TIME_STEP * pull
            bodies[3 + i] = velocity
            bodies[i] = bodies[i] + TIME_STEP * velocity

    def send_migrants(step):
        hot = lane_hot[step]
        parts = split3(bodies[...].reshape(7 * NBLK, 128))
        picked = jnp.dot(parts[0], hot, preferred_element_type=F32)
        picked = picked + jnp.dot(parts[1], hot, preferred_element_type=F32)
        picked = picked + jnp.dot(parts[2], hot, preferred_element_type=F32)
        hit = block_hot[step, 0] > 0.5
        for row in range(7):
            line = jnp.where(hit, picked[NBLK * row : NBLK * row + NBLK], 0.0)
            line = jnp.sum(line, axis=0, keepdims=True)
            outgoing[step, 0, row : row + 1, :] = line[:, 0:128]
            outgoing[step, 1, row : row + 1, :] = line[:, 128:256]
        for half in range(2):
            outgoing[step, half, 7:8, :] = jnp.zeros((1, 128), F32)

        def send(hop, carry):
            mig_copy(step, hop).start()
            return carry

        lax.fori_loop(1, GROUP, send, 0)

    def take_migrants(step):
        def wait(hop, carry):
            mig_copy(step, hop).wait_recv()
            return carry

        lax.fori_loop(1, GROUP, wait, 0)
        place = lax.shift_right_logical(lax.broadcasted_iota(jnp.int32, (8, 128), 1), 4)
        shift = (me % 8) * 16
        halves = []
        for half in range(2):
            whole = jnp.zeros((8, 128), F32)
            for spot in range(8):
                turned = pltpu.roll(
                    arrived[step, 8 * half + spot], lax.rem(16 * spot + 128 - shift, 128), axis=1
                )
                whole = jnp.where(place == spot, turned, whole)
            halves.append(whole)
        values = jnp.concatenate(halves, axis=1)
        filled = block_hot[step, 1] > 0.5
        spread = jnp.concatenate(
            [jnp.where(filled, values[row : row + 1, :], 0.0) for row in range(7)], axis=0
        )
        dims = (((1,), (1,)), ((), ()))
        hot = lane_hot[step]
        landed = jnp.zeros((7 * NBLK, 128), F32)
        for part in split3(spread):
            landed = landed + lax.dot_general(part, hot, dims, preferred_element_type=F32)
        hits = lax.dot_general(
            block_hot[step, 1].astype(BF16), hot, dims, preferred_element_type=F32
        )
        for row in range(7):
            bodies[row] = jnp.where(hits > 0.5, landed[NBLK * row : NBLK * row + NBLK], bodies[row])

    for step in range(STEPS):
        for face, (lender, _, _) in enumerate(faces):
            @pl.when(jnp.logical_not(lender))
            def _():
                pool[step][pl.ds(NBLK + GHOST * face, GHOST)] = jnp.zeros((GHOST, 8, 128), F32)
        arrived[step, me] = jnp.zeros((8, 128), F32)

    for load in loads:
        load.wait()
    neighbours = 20 + (gx > 0).astype(jnp.int32) + (gx < SLABS - 1).astype(jnp.int32)
    pl.semaphore_wait(barrier, neighbours)

    for step in range(STEPS):
        send_ghosts(step)
        if step == 0:
            start_tri(0)
            prepare()
            wait_ghosts(0)
            forward_tri(0)
            start_tri(1)
            pair_forces(0)
            finish_tri(0)
            forward_tri(1)
            start_tri(2)
            wait_tri(0)
            wall_forces(0)
            finish_tri(1)
            forward_tri(2)
        else:
            if step == 1:
                wait_tri(1)
            else:
                wait_tri(2)
            wall_forces(step)
            if step == 1:
                finish_tri(2)
            wait_ghosts(step)
            pair_forces(step)
        integrate()
        send_migrants(step)
        take_migrants(step)

    stores = [
        pltpu.make_async_copy(bodies.at[pl.ds(0, 3)], pos_o, in_sem.at[2]),
        pltpu.make_async_copy(bodies.at[pl.ds(3, 3)], vel_o, in_sem.at[3]),
        pltpu.make_async_copy(bodies.at[6], rad_o, in_sem.at[4]),
    ]
    for store in stores:
        store.start()
    for step in range(STEPS):
        for face, (_, borrower, target) in enumerate(faces):
            @pl.when(borrower)
            def _():
                ghost_copy(step, face, target).wait_send()
        zh_copy(step).wait_send()
        for hop in (1, 2, 3):
            x_copy(step, hop).wait_send()
            xz_copy(step, hop).wait_send()
        for slot in range(8):
            core_copy(step, gx, slot).wait_send()

        def wait(hop, carry):
            mig_copy(step, hop).wait_send()
            return carry

        lax.fori_loop(1, GROUP, wait, 0)
    for store in stores:
        store.wait()


def shards(
    position, velocity, radius, vertices, vertex_speed, angles, ghost_blocks,
    tile_home, tile_other, wall_home, wall_block, mig_order, mig_count,
):
    whole = pl.BlockSpec(memory_space=pl.ANY)
    scalars = pl.BlockSpec(memory_space=pltpu.SMEM)
    dma = pltpu.SemaphoreType.DMA
    out = pl.pallas_call(
        kernel,
        out_shape=(
            jax.ShapeDtypeStruct((3, NBLK, 128), F32),
            jax.ShapeDtypeStruct((3, NBLK, 128), F32),
            jax.ShapeDtypeStruct((NBLK, 128), F32),
        ),
        in_specs=[whole] * 6 + [scalars] * 7,
        out_specs=(whole, whole, whole),
        scratch_shapes=[
            pltpu.VMEM((7, NBLK, 128), F32),
            pltpu.VMEM((9, TRIBLK, 128), F32),
            pltpu.VMEM((9, TRIBLK, 128), F32),
            pltpu.VMEM((STEPS, 8, 128), jnp.int32),
            pltpu.VMEM((NBLK, 8, 128), F32),
            *[pltpu.VMEM((POOL, 8, 128), F32) for _ in range(STEPS)],
            pltpu.VMEM((STEPS, GHOST, 8, 128), F32),
            *[pltpu.VMEM((SLABS * TRIBLK, 8, 128), F32) for _ in range(STEPS)],
            pltpu.VMEM((STEPS, 2, 8, 128), F32),
            pltpu.VMEM((STEPS, GROUP, 8, 128), F32),
            pltpu.VMEM((STEPS, 128, 256), BF16),
            pltpu.VMEM((STEPS, 2, NBLK, 256), F32),
            pltpu.VMEM((TILES, 128), F32),
            pltpu.VMEM((TTILES, 128), F32),
            pltpu.VMEM((3, TILES, 128), F32),
            pltpu.VMEM((3, TTILES, 128), F32),
            dma((6,)),
            dma((STEPS, 6)),
            dma((STEPS, 6)),
            dma((STEPS, GROUP)),
            dma((STEPS, GROUP)),
            dma((STEPS,)),
            dma((STEPS,)),
            dma((STEPS, 3)),
            dma((STEPS, 3)),
            dma((STEPS, 3)),
            dma((STEPS, 3)),
            dma((STEPS, 8)),
            dma((STEPS, 8)),
        ],
        compiler_params=pltpu.CompilerParams(
            collective_id=0, has_side_effects=True, vmem_limit_bytes=32 * 1024 * 1024
        ),
    )(
        position.reshape(3, NBLK, 128),
        velocity.reshape(3, NBLK, 128),
        radius.reshape(NBLK, 128),
        vertices.reshape(9, TRIBLK, 128),
        vertex_speed.reshape(9, TRIBLK, 128),
        mig_order.reshape(STEPS, NBLK, 128),
        angles,
        ghost_blocks.reshape(-1),
        tile_home.reshape(-1),
        tile_other.reshape(-1),
        wall_home.reshape(-1),
        wall_block.reshape(-1),
        mig_count.reshape(STEPS, GROUP),
    )
    return (
        out[0].reshape(position.shape),
        out[1].reshape(velocity.shape),
        out[2].reshape(radius.shape),
    )


def solution(mesh):
    block = P("gx", "gy", "gz", None)
    blocks = P(None, "gx", "gy", "gz", None)
    in_specs = (
        blocks, blocks, block, blocks, blocks, P(), block, block, block, block, block, blocks, blocks,
    )
    return jax.shard_map(
        shards, mesh=mesh, in_specs=in_specs, out_specs=(blocks, blocks, block), check_vma=False
    )
```

```python
import functools

import jax
import jax.numpy as jnp
from jax import lax
from jax.experimental import pallas as pl
from jax.experimental.pallas import tpu as pltpu
from jax.sharding import PartitionSpec as P

MESH = pl.DeviceIdType.MESH
F32 = jnp.float32
BF16 = jnp.bfloat16

STEPS = 3
NBLK = 32
GHOST = 16
POOL = 128
TILES = 64
TTILES = 32
TRIBLK = 16
SLABS = 16
GROUP = 16
MC = 16
SOME = 8

STIFFNESS = 20.0
DAMPING = 2.0
WALL_STIFF = 20.0
SOFTENING = 0.01
TIME_STEP = 0.02
GRAVITY = 1.0
AXIS_CENTRE = 2.0
AREA_FLOOR = 1.0
SPREAD_PAD = 0.25


def split3(values):
    high = values.astype(BF16)
    rest = values - high.astype(F32)
    middle = rest.astype(BF16)
    low = (rest - middle.astype(F32)).astype(BF16)
    return high, middle, low


def split2(values):
    high = values.astype(BF16)
    low = (values - high.astype(F32)).astype(BF16)
    return high, low


def split3_wide(values):
    high = values.astype(BF16).astype(F32)
    rest = values - high
    middle = rest.astype(BF16).astype(F32)
    return high, middle, rest - middle


def swapped(block, row):
    return jnp.where(row < 3, pltpu.roll(block, 5, axis=0), pltpu.roll(block, 3, axis=0))


def over_rows(values, mask):
    total = jnp.sum(jnp.where(mask, values, 0.0), axis=0, keepdims=True)
    return jnp.broadcast_to(total, (8, 128))


def by_row(row, values):
    out = values[-1]
    for i in range(len(values) - 2, -1, -1):
        out = jnp.where(row == i, values[i], out)
    return out


def stacked(groups):
    return jnp.concatenate(groups, axis=0)


def anchor_of(home, row):
    return jnp.where(row < 6, jnp.broadcast_to(home[:, 0:1], (8, 128)), 0.0)


def pair_home(home, row):
    block = home - anchor_of(home, row)
    turned = swapped(block, row)
    norm = split3_wide(over_rows(block * block, row < 3) + SOFTENING)
    drift = split3_wide(-DAMPING * over_rows(block * turned, row < 3))
    size = split3_wide(jnp.broadcast_to(block[6:7], (8, 128)))
    zero, one = jnp.zeros((8, 128), F32), jnp.ones((8, 128), F32)
    near = [jnp.where(row < 3, -2.0 * part, 0.0) for part in split3_wide(block)]
    cross = [jnp.where(row < 6, DAMPING * part, 0.0) for part in split3_wide(turned)]
    six = (row == 6).astype(F32)
    near_end = by_row(row, [one, one, one, zero, zero, norm[0], norm[1], norm[2]])
    cross_end = by_row(
        row, [zero, zero, zero, -DAMPING * one, -DAMPING * one, drift[0], drift[1], drift[2]]
    )
    size_end = by_row(row, [zero, zero, zero, zero, zero, size[0], size[1], size[2]])
    return jnp.concatenate(
        [
            stacked([near[0], near[1], near[0], near[1], near[2], near[0], near_end, zero]),
            stacked([cross[0], cross[1], cross[0], cross[1], cross[2], cross[0], cross_end, zero]),
            stacked([six, zero, six, zero, zero, six, size_end, zero]),
        ],
        axis=1,
    ).astype(BF16)


def low_below(weights, row):
    high = weights.astype(BF16).astype(F32)
    return jnp.where(row < 4, high, pltpu.roll(weights - high, 4, axis=0)).astype(BF16)


def pair_other(other, home, row):
    block = other - anchor_of(home, row)
    turned = swapped(block, row)
    norm = split3_wide(over_rows(block * block, row < 3))
    drift = over_rows(block * turned, row < 3)
    drift_high = drift.astype(BF16).astype(F32)
    one = jnp.ones((8, 128), F32)
    end = by_row(row, [norm[0], norm[1], norm[2], drift_high, drift - drift_high, one, one, one])
    part = split3_wide(block)
    left = stacked(
        [part[0], part[0], part[1], part[1], part[0], part[2], end, jnp.zeros((8, 128), F32)]
    ).astype(BF16)
    weights = jnp.where(row < 3, block, 1.0) * jnp.broadcast_to(block[6:7], (8, 128))
    return left, low_below(weights, row)


def wall_home(home, row):
    block = home - AXIS_CENTRE
    norm = split3_wide(-over_rows(block * block, row < 3))
    parts = split3_wide(block)
    zero = jnp.zeros((8, 128), F32)
    high = [jnp.where(row < 3, part, 0.0) for part in parts]
    wide = [
        jnp.where(jnp.logical_and(row >= 3, row < 6), 2.0 * pltpu.roll(part, 3, axis=0), 0.0)
        for part in parts
    ]
    level = jnp.where(row == 7, -1.0, 0.0)
    six = (row == 6).astype(F32)
    end = by_row(row, [norm[0], norm[1], norm[2], zero])
    return jnp.concatenate(
        [
            stacked([high[0] + level, high[1], high[0] + level, high[1], high[2], high[0] + level, zero, zero]),
            stacked([wide[0] + six, wide[1], wide[0] + six, wide[1], wide[2], wide[0] + six, end, zero]),
        ],
        axis=1,
    ).astype(BF16)


def wall_other(blades, row):
    part = split3_wide(blades)
    end = jnp.where(row < 3, 1.0, 0.0)
    left = stacked(
        [part[0], part[0], part[1], part[1], part[0], part[2], end, jnp.zeros((8, 128), F32)]
    ).astype(BF16)
    reach = over_rows(blades * blades, jnp.logical_and(row >= 3, row < 6))
    weights = blades / (reach + jnp.broadcast_to(blades[6:7], (8, 128)))
    return left, low_below(weights, row)


def weighted(weights, strength):
    high, low = split2(strength)
    return jnp.dot(
        jnp.concatenate([weights, weights], axis=1),
        jnp.concatenate([high, low], axis=0),
        preferred_element_type=F32,
    )


def kernel(
    pos_h, vel_h, rad_h, vert_h, speed_h, order_h, angles, ghost_ids, home_ids, other_ids,
    wall_ids, wall_picks, counts,
    pos_o, vel_o, rad_o,
    bodies, corners, speeds, order, own, pool_0, pool_1, pool_2, lent, tri_0, tri_1, tri_2,
    outgoing, arrived, lane_hot, block_hot,
    pair_sel, wall_sel, pair_out, wall_out,
    pair_right, pair_left, pair_weight, wall_right, wall_left, wall_weight,
    in_sem, ghost_send, ghost_recv, mig_send, mig_recv,
    zh_send, zh_recv, x_send, x_recv, xz_send, xz_recv, core_send, core_recv,
):
    pool, tri = (pool_0, pool_1, pool_2), (tri_0, tri_1, tri_2)
    gx = lax.axis_index("gx")
    gy = lax.axis_index("gy")
    gz = lax.axis_index("gz")
    me = gy * 4 + gz
    x_at, zh, core = gx // 4, (gx // 2) % 2, gx % 2
    twin = gx + 1 - 2 * core
    zmate = gx + 2 - 4 * zh

    loads = [
        pltpu.make_async_copy(vert_h, corners, in_sem.at[0]),
        pltpu.make_async_copy(speed_h, speeds, in_sem.at[1]),
        pltpu.make_async_copy(pos_h, bodies.at[pl.ds(0, 3)], in_sem.at[2]),
        pltpu.make_async_copy(vel_h, bodies.at[pl.ds(3, 3)], in_sem.at[3]),
        pltpu.make_async_copy(rad_h, bodies.at[6], in_sem.at[4]),
        pltpu.make_async_copy(order_h.at[:, pl.ds(0, 8), :], order, in_sem.at[5]),
    ]
    for load in loads:
        load.start()

    def peer_of(hop):
        peer = lax.rem(me + hop, GROUP)
        return peer, (gx, peer // 4, peer % 4)

    def x_mate(hop, z_of):
        index = lax.rem(x_at + hop, 4) * 4 + z_of * 2 + core
        return index

    faces = [
        (gx > 0, gx < SLABS - 1, (gx + 1, gy, gz)),
        (gx < SLABS - 1, gx > 0, (gx - 1, gy, gz)),
        (gy > 0, gy < 3, (gx, gy + 1, gz)),
        (gy < 3, gy > 0, (gx, gy - 1, gz)),
        (gz > 0, gz < 3, (gx, gy, gz + 1)),
        (gz < 3, gz > 0, (gx, gy, gz - 1)),
    ]

    barrier = pltpu.get_barrier_semaphore()

    def greet(hop, carry):
        pl.semaphore_signal(barrier, inc=1, device_id=peer_of(hop)[1], device_id_type=MESH)
        return carry

    lax.fori_loop(1, GROUP, greet, 0)
    for other in (twin, zmate, x_mate(1, zh), x_mate(2, zh), x_mate(3, zh)):
        pl.semaphore_signal(barrier, inc=1, device_id=(other, gy, gz), device_id_type=MESH)
    for _, borrower, target in faces[:2]:
        @pl.when(borrower)
        def _():
            pl.semaphore_signal(barrier, inc=1, device_id=target, device_id_type=MESH)

    def ghost_copy(step, face, target):
        return pltpu.make_async_remote_copy(
            src_ref=lent.at[step],
            dst_ref=pool[step].at[pl.ds(NBLK + GHOST * face, GHOST)],
            send_sem=ghost_send.at[step, face],
            recv_sem=ghost_recv.at[step, face],
            device_id=target,
            device_id_type=MESH,
        )

    def tri_copy(step, owner, target, send, recv):
        part = tri[step].at[pl.ds(owner * TRIBLK, TRIBLK)]
        return pltpu.make_async_remote_copy(
            src_ref=part,
            dst_ref=part,
            send_sem=send,
            recv_sem=recv,
            device_id=(target, gy, gz),
            device_id_type=MESH,
        )

    def zh_copy(step):
        return tri_copy(step, gx, zmate, zh_send.at[step], zh_recv.at[step])

    def core_copy(step, owner, slot):
        return tri_copy(step, owner, twin, core_send.at[step, slot], core_recv.at[step, slot])

    def x_copy(step, hop):
        return tri_copy(step, gx, x_mate(hop, zh), x_send.at[step, hop - 1], x_recv.at[step, hop - 1])

    def xz_copy(step, hop):
        return tri_copy(step, zmate, x_mate(hop, zh), xz_send.at[step, hop - 1], xz_recv.at[step, hop - 1])

    def mig_copy(step, hop):
        peer, target = peer_of(hop)
        return pltpu.make_async_remote_copy(
            src_ref=outgoing.at[step, peer // 8],
            dst_ref=arrived.at[step, me],
            send_sem=mig_send.at[step, hop],
            recv_sem=mig_recv.at[step, hop],
            device_id=target,
            device_id_type=MESH,
        )

    def lend(step):
        for row in range(7):
            own[:, row, :] = bodies[row]
        own[:, 7, :] = jnp.zeros((NBLK, 128), F32)
        for slot in range(GHOST):
            lent[step, slot] = own[ghost_ids[slot]]

    def send_ghosts(step):
        for face, (_, borrower, target) in enumerate(faces):
            @pl.when(borrower)
            def _():
                ghost_copy(step, face, target).start()
        pool[step][pl.ds(0, NBLK)] = own[...]

    def wait_ghosts(step):
        for face, (lender, _, target) in enumerate(faces):
            @pl.when(lender)
            def _():
                ghost_copy(step, face, target).wait_recv()

    def blade_move(step):
        angle = jnp.full((8, 128), angles[step], F32)
        cosine = jnp.cos(angle)[0:1]
        sine = jnp.sin(angle)[0:1]
        now = []
        for corner in range(3):
            along = corners[3 * corner]
            rel_y = corners[3 * corner + 1] - AXIS_CENTRE
            rel_z = corners[3 * corner + 2] - AXIS_CENTRE
            for j, value in enumerate((
                along,
                AXIS_CENTRE + cosine * rel_y - sine * rel_z,
                AXIS_CENTRE + sine * rel_y + cosine * rel_z,
            )):
                moved = value + TIME_STEP * speeds[3 * corner + j]
                corners[3 * corner + j] = moved
                now.append(moved)
        a, b, c = now[0:3], now[3:6], now[6:9]
        centre = [(a[i] + b[i] + c[i]) / 3.0 for i in range(3)]
        u = [b[i] - a[i] for i in range(3)]
        w = [c[i] - a[i] for i in range(3)]
        area = [
            u[1] * w[2] - u[2] * w[1],
            u[2] * w[0] - u[0] * w[2],
            u[0] * w[1] - u[1] * w[0],
        ]
        length = jnp.sqrt(area[0] * area[0] + area[1] * area[1] + area[2] * area[2])
        scale = 1.0 / jnp.maximum(length, AREA_FLOOR)
        normal = [area[i] * scale for i in range(3)]
        spread = SPREAD_PAD
        for corner in (a, b, c):
            for i in range(3):
                spread = spread + (corner[i] - centre[i]) ** 2 * (1.0 / 3.0)
        shifted = [centre[i] - AXIS_CENTRE for i in range(3)]
        square = shifted[0] ** 2 + shifted[1] ** 2 + shifted[2] ** 2
        level = normal[0] * shifted[0] + normal[1] * shifted[1] + normal[2] * shifted[2]
        rows = normal + shifted + [spread - square, level]
        for row in range(8):
            tri[step][pl.ds(gx * TRIBLK, TRIBLK), row, :] = rows[row]

    def start_tri(step):
        zh_copy(step).start()
        core_copy(step, gx, 0).start()
        for hop in (1, 2, 3):
            x_copy(step, hop).start()

    def forward_tri(step):
        zh_copy(step).wait_recv()
        for hop in (1, 2, 3):
            xz_copy(step, hop).start()
        core_copy(step, zmate, 1).start()

    def finish_tri(step):
        for hop in (1, 2, 3):
            x_copy(step, hop).wait_recv()
            core_copy(step, x_mate(4 - hop, zh), 1 + hop).start()
        for hop in (1, 2, 3):
            xz_copy(step, hop).wait_recv()
            core_copy(step, x_mate(4 - hop, 1 - zh), 4 + hop).start()

    def wait_tri(step):
        for slot in range(8):
            core_copy(step, gx, slot).wait_recv()

    def prepare():
        lane = lax.broadcasted_iota(jnp.int32, (128, 256), 0)
        block = lax.broadcasted_iota(jnp.int32, (NBLK, 256), 0)
        place = lax.broadcasted_iota(jnp.int32, (1, 256), 1)
        for step in range(STEPS):
            ids = jnp.concatenate([order[step, 0:1, :], order[step, 1:2, :]], axis=1)
            lane_hot[step] = (jnp.bitwise_and(ids, 127) == lane).astype(F32).astype(BF16)
            limit = jnp.zeros((1, 256), jnp.int32)
            for peer in range(GROUP):
                limit = jnp.where(lax.shift_right_logical(place, 4) == peer, counts[step, 0, peer], limit)
            filled = jnp.bitwise_and(place, 15) < limit
            hot = lax.shift_right_logical(ids, 7) == block
            block_hot[step, 0] = hot.astype(F32)
            block_hot[step, 1] = jnp.logical_and(hot, filled).astype(F32)
        home = lax.broadcasted_iota(jnp.int32, (1, 128), 1)
        hot = [(home == home_ids[tile]).astype(F32) for tile in range(TILES)]
        pair_sel[...] = stacked(hot).T[0:NBLK].astype(BF16)
        hot = [(home == wall_ids[tile]).astype(F32) for tile in range(TTILES)]
        wall_sel[...] = stacked(hot).T[0:NBLK].astype(BF16)

    def pair_homes():
        def some(turn, carry):
            row = lax.broadcasted_iota(jnp.int32, (8, 128), 0)
            for spot in range(SOME):
                tile = turn * SOME + spot
                pair_right[tile] = pair_home(own[home_ids[tile]], row)
            return carry

        lax.fori_loop(0, TILES // SOME, some, 0)

    def pair_forces(step):
        def features(turn, carry):
            row = lax.broadcasted_iota(jnp.int32, (8, 128), 0)
            for spot in range(SOME):
                tile = turn * SOME + spot
                left, weights = pair_other(pool[step][other_ids[tile]], own[home_ids[tile]], row)
                pair_left[tile] = left.T
                pair_weight[tile] = weights
            return carry

        def forces(turn, carry):
            tiles = [turn * SOME + spot for spot in range(SOME)]
            forms = [
                jnp.dot(pair_left[tile], pair_right[tile], preferred_element_type=F32)
                for tile in tiles
            ]
            strengths = []
            for form in forms:
                square = jnp.maximum(form[:, 0:128], SOFTENING)
                speed, reach = form[:, 128:256], form[:, 256:384]
                scaled = square * reach
                ratio = lax.rsqrt(scaled * reach)
                overlap = jnp.maximum(reach - scaled * ratio, 0.0)
                strengths.append(overlap * ratio * (STIFFNESS + speed * (reach * ratio)))
            for tile, strength in zip(tiles, strengths):
                pair_out[tile] = weighted(pair_weight[tile], strength)
            return carry

        lax.fori_loop(0, TILES // SOME, features, 0)
        lax.fori_loop(0, TILES // SOME, forces, 0)

    def wall_forces(step):
        def features(turn, carry):
            row = lax.broadcasted_iota(jnp.int32, (8, 128), 0)
            for spot in range(SOME):
                tile = turn * SOME + spot
                wall_right[tile] = wall_home(own[wall_ids[tile]], row)
                left, weights = wall_other(tri[step][wall_picks[tile]], row)
                wall_left[tile] = left.T
                wall_weight[tile] = weights
            return carry

        def forces(turn, carry):
            tiles = [turn * SOME + spot for spot in range(SOME)]
            forms = [
                jnp.dot(wall_left[tile], wall_right[tile], preferred_element_type=F32)
                for tile in tiles
            ]
            strengths = []
            for tile, form in zip(tiles, forms):
                radius = own[wall_ids[tile]][6:7, :]
                height, window = form[:, 0:128], form[:, 128:256]
                depth = jnp.maximum(radius - jnp.abs(height), 0.0)
                strengths.append(depth * height * jnp.maximum(window, 0.0))
            for tile, strength in zip(tiles, strengths):
                wall_out[tile] = weighted(wall_weight[tile], strength)
            return carry

        lax.fori_loop(0, TTILES // SOME, features, 0)
        lax.fori_loop(0, TTILES // SOME, forces, 0)

    def integrate():
        def home_sum(select, out, row):
            high, low = split2(out[:, row, :] + out[:, row + 4, :])
            return jnp.dot(select, high, preferred_element_type=F32) + jnp.dot(
                select, low, preferred_element_type=F32
            )

        pairs, walls = pair_sel[...], wall_sel[...]
        weight = home_sum(pairs, pair_out, 3)
        radius = bodies[6]
        inertia = 1.0 / (radius * radius)
        for i in range(3):
            place = bodies[i]
            contact = (place - place[:, 0:1]) * weight - home_sum(pairs, pair_out, i)
            pull = (contact + WALL_STIFF * home_sum(walls, wall_out, i)) * inertia
            if i == 2:
                pull = pull - GRAVITY
            velocity = bodies[3 + i] + TIME_STEP * pull
            bodies[3 + i] = velocity
            bodies[i] = place + TIME_STEP * velocity

    def send_migrants(step):
        hot = lane_hot[step]
        parts = split3(bodies[...].reshape(7 * NBLK, 128))
        picked = jnp.dot(parts[0], hot, preferred_element_type=F32)
        picked = picked + jnp.dot(parts[1], hot, preferred_element_type=F32)
        picked = picked + jnp.dot(parts[2], hot, preferred_element_type=F32)
        hit = block_hot[step, 0] > 0.5
        for row in range(7):
            line = jnp.where(hit, picked[NBLK * row : NBLK * row + NBLK], 0.0)
            line = jnp.sum(line, axis=0, keepdims=True)
            outgoing[step, 0, row : row + 1, :] = line[:, 0:128]
            outgoing[step, 1, row : row + 1, :] = line[:, 128:256]
        for half in range(2):
            outgoing[step, half, 7:8, :] = jnp.zeros((1, 128), F32)

        def send(hop, carry):
            mig_copy(step, hop).start()
            return carry

        lax.fori_loop(1, GROUP, send, 0)

    def take_migrants(step):
        def wait(hop, carry):
            mig_copy(step, hop).wait_recv()
            return carry

        lax.fori_loop(1, GROUP, wait, 0)
        place = lax.shift_right_logical(lax.broadcasted_iota(jnp.int32, (8, 128), 1), 4)
        shift = (me % 8) * 16
        halves = []
        for half in range(2):
            whole = jnp.zeros((8, 128), F32)
            for spot in range(8):
                turned = pltpu.roll(
                    arrived[step, 8 * half + spot], lax.rem(16 * spot + 128 - shift, 128), axis=1
                )
                whole = jnp.where(place == spot, turned, whole)
            halves.append(whole)
        values = jnp.concatenate(halves, axis=1)
        filled = block_hot[step, 1] > 0.5
        spread = jnp.concatenate(
            [jnp.where(filled, values[row : row + 1, :], 0.0) for row in range(7)], axis=0
        )
        dims = (((1,), (1,)), ((), ()))
        hot = lane_hot[step]
        landed = jnp.zeros((7 * NBLK, 128), F32)
        for part in split3(spread):
            landed = landed + lax.dot_general(part, hot, dims, preferred_element_type=F32)
        hits = lax.dot_general(
            block_hot[step, 1].astype(BF16), hot, dims, preferred_element_type=F32
        )
        for row in range(7):
            bodies[row] = jnp.where(hits > 0.5, landed[NBLK * row : NBLK * row + NBLK], bodies[row])

    for step in range(STEPS):
        for face, (lender, _, _) in enumerate(faces):
            @pl.when(jnp.logical_not(lender))
            def _():
                pool[step][pl.ds(NBLK + GHOST * face, GHOST)] = jnp.zeros((GHOST, 8, 128), F32)
        arrived[step, me] = jnp.zeros((8, 128), F32)

    for load in loads:
        load.wait()
    lend(0)
    blade_move(0)
    neighbours = 20 + (gx > 0).astype(jnp.int32) + (gx < SLABS - 1).astype(jnp.int32)
    pl.semaphore_wait(barrier, neighbours)

    for step in range(STEPS):
        if step > 0:
            lend(step)
        send_ghosts(step)
        if step == 0:
            start_tri(0)
            pair_homes()
            blade_move(1)
            blade_move(2)
            prepare()
            forward_tri(0)
            start_tri(1)
            wait_ghosts(0)
            pair_forces(0)
            finish_tri(0)
            forward_tri(1)
            start_tri(2)
            wait_tri(0)
            wall_forces(0)
            finish_tri(1)
            forward_tri(2)
        else:
            pair_homes()
            wait_tri(step)
            wall_forces(step)
            if step == 1:
                finish_tri(2)
            wait_ghosts(step)
            pair_forces(step)
        integrate()
        send_migrants(step)
        take_migrants(step)

    stores = [
        pltpu.make_async_copy(bodies.at[pl.ds(0, 3)], pos_o, in_sem.at[2]),
        pltpu.make_async_copy(bodies.at[pl.ds(3, 3)], vel_o, in_sem.at[3]),
        pltpu.make_async_copy(bodies.at[6], rad_o, in_sem.at[4]),
    ]
    for store in stores:
        store.start()
    for step in range(STEPS):
        for face, (_, borrower, target) in enumerate(faces):
            @pl.when(borrower)
            def _():
                ghost_copy(step, face, target).wait_send()
        zh_copy(step).wait_send()
        for hop in (1, 2, 3):
            x_copy(step, hop).wait_send()
            xz_copy(step, hop).wait_send()
        for slot in range(8):
            core_copy(step, gx, slot).wait_send()

        def wait(hop, carry):
            mig_copy(step, hop).wait_send()
            return carry

        lax.fori_loop(1, GROUP, wait, 0)
    for store in stores:
        store.wait()


def shards(
    position, velocity, radius, vertices, vertex_speed, angles, ghost_blocks,
    tile_home, tile_other, wall_home, wall_block, mig_order, mig_count,
):
    whole = pl.BlockSpec(memory_space=pl.ANY)
    scalars = pl.BlockSpec(memory_space=pltpu.SMEM)
    dma = pltpu.SemaphoreType.DMA
    out = pl.pallas_call(
        kernel,
        out_shape=(
            jax.ShapeDtypeStruct((3, NBLK, 128), F32),
            jax.ShapeDtypeStruct((3, NBLK, 128), F32),
            jax.ShapeDtypeStruct((NBLK, 128), F32),
        ),
        in_specs=[whole] * 6 + [scalars] * 7,
        out_specs=(whole, whole, whole),
        scratch_shapes=[
            pltpu.VMEM((7, NBLK, 128), F32),
            pltpu.VMEM((9, TRIBLK, 128), F32),
            pltpu.VMEM((9, TRIBLK, 128), F32),
            pltpu.VMEM((STEPS, 8, 128), jnp.int32),
            pltpu.VMEM((NBLK, 8, 128), F32),
            *[pltpu.VMEM((POOL, 8, 128), F32) for _ in range(STEPS)],
            pltpu.VMEM((STEPS, GHOST, 8, 128), F32),
            *[pltpu.VMEM((SLABS * TRIBLK, 8, 128), F32) for _ in range(STEPS)],
            pltpu.VMEM((STEPS, 2, 8, 128), F32),
            pltpu.VMEM((STEPS, GROUP, 8, 128), F32),
            pltpu.VMEM((STEPS, 128, 256), BF16),
            pltpu.VMEM((STEPS, 2, NBLK, 256), F32),
            pltpu.VMEM((NBLK, TILES), BF16),
            pltpu.VMEM((NBLK, TTILES), BF16),
            pltpu.VMEM((TILES, 8, 128), F32),
            pltpu.VMEM((TTILES, 8, 128), F32),
            pltpu.VMEM((TILES, 64, 384), BF16),
            pltpu.VMEM((TILES, 128, 64), BF16),
            pltpu.VMEM((TILES, 8, 128), BF16),
            pltpu.VMEM((TTILES, 64, 256), BF16),
            pltpu.VMEM((TTILES, 128, 64), BF16),
            pltpu.VMEM((TTILES, 8, 128), BF16),
            dma((6,)),
            dma((STEPS, 6)),
            dma((STEPS, 6)),
            dma((STEPS, GROUP)),
            dma((STEPS, GROUP)),
            dma((STEPS,)),
            dma((STEPS,)),
            dma((STEPS, 3)),
            dma((STEPS, 3)),
            dma((STEPS, 3)),
            dma((STEPS, 3)),
            dma((STEPS, 8)),
            dma((STEPS, 8)),
        ],
        compiler_params=pltpu.CompilerParams(
            collective_id=0, has_side_effects=True, vmem_limit_bytes=60 * 1024 * 1024
        ),
    )(
        position.reshape(3, NBLK, 128),
        velocity.reshape(3, NBLK, 128),
        radius.reshape(NBLK, 128),
        vertices.reshape(9, TRIBLK, 128),
        vertex_speed.reshape(9, TRIBLK, 128),
        mig_order.reshape(STEPS, NBLK, 128),
        angles,
        ghost_blocks.reshape(-1),
        tile_home.reshape(-1),
        tile_other.reshape(-1),
        wall_home.reshape(-1),
        wall_block.reshape(-1),
        mig_count.reshape(STEPS, 1, GROUP),
    )
    return (
        out[0].reshape(position.shape),
        out[1].reshape(velocity.shape),
        out[2].reshape(radius.shape),
    )


def solution(mesh):
    block = P("gx", "gy", "gz", None)
    blocks = P(None, "gx", "gy", "gz", None)
    in_specs = (
        blocks, blocks, block, blocks, blocks, P(), block, block, block, block, block, blocks, blocks,
    )
    return jax.shard_map(
        shards, mesh=mesh, in_specs=in_specs, out_specs=(blocks, blocks, block), check_vma=False
    )
```

```python
import functools

import jax
import jax.numpy as jnp
from jax import lax
from jax.experimental import pallas as pl
from jax.experimental.pallas import tpu as pltpu
from jax.sharding import PartitionSpec as P

MESH = pl.DeviceIdType.MESH
F32 = jnp.float32
BF16 = jnp.bfloat16

STEPS = 3
NBLK = 32
GHOST = 16
POOL = 128
TILES = 64
TTILES = 32
TRIBLK = 16
SLABS = 16
GROUP = 16
MC = 16
SOME = 32

STIFFNESS = 20.0
DAMPING = 2.0
WALL_STIFF = 20.0
SOFTENING = 0.01
TIME_STEP = 0.02
GRAVITY = 1.0
AXIS_CENTRE = 2.0
AREA_FLOOR = 1.0
SPREAD_PAD = 0.25


def split3(values):
    high = values.astype(BF16)
    rest = values - high.astype(F32)
    middle = rest.astype(BF16)
    low = (rest - middle.astype(F32)).astype(BF16)
    return high, middle, low


def split2(values):
    high = values.astype(BF16)
    low = (values - high.astype(F32)).astype(BF16)
    return high, low


def split3_wide(values):
    high = values.astype(BF16).astype(F32)
    rest = values - high
    middle = rest.astype(BF16).astype(F32)
    return high, middle, rest - middle


def swapped(block, row):
    return jnp.where(row < 3, pltpu.roll(block, 5, axis=0), pltpu.roll(block, 3, axis=0))


def over_rows(values, mask):
    total = jnp.sum(jnp.where(mask, values, 0.0), axis=0, keepdims=True)
    return jnp.broadcast_to(total, (8, 128))


def by_row(row, values):
    out = values[-1]
    for i in range(len(values) - 2, -1, -1):
        out = jnp.where(row == i, values[i], out)
    return out


def stacked(groups):
    return jnp.concatenate(groups, axis=0)


def anchor_of(home, row):
    return jnp.where(row < 6, jnp.broadcast_to(home[:, 0:1], (8, 128)), 0.0)


def pair_home(home, row):
    block = home - anchor_of(home, row)
    turned = swapped(block, row)
    norm = split3_wide(over_rows(block * block, row < 3) + SOFTENING)
    drift = split3_wide(-DAMPING * over_rows(block * turned, row < 3))
    size = split3_wide(jnp.broadcast_to(block[6:7], (8, 128)))
    zero, one = jnp.zeros((8, 128), F32), jnp.ones((8, 128), F32)
    near = [jnp.where(row < 3, -2.0 * part, 0.0) for part in split3_wide(block)]
    cross = [jnp.where(row < 6, DAMPING * part, 0.0) for part in split3_wide(turned)]
    six = (row == 6).astype(F32)
    near_end = by_row(row, [one, one, one, zero, zero, norm[0], norm[1], norm[2]])
    cross_end = by_row(
        row, [zero, zero, zero, -DAMPING * one, -DAMPING * one, drift[0], drift[1], drift[2]]
    )
    size_end = by_row(row, [zero, zero, zero, zero, zero, size[0], size[1], size[2]])
    return jnp.concatenate(
        [
            stacked([near[0], near[1], near[0], near[1], near[2], near[0], near_end, zero]),
            stacked([cross[0], cross[1], cross[0], cross[1], cross[2], cross[0], cross_end, zero]),
            stacked([six, zero, six, zero, zero, six, size_end, zero]),
        ],
        axis=1,
    ).astype(BF16)


def low_below(weights, row):
    high = weights.astype(BF16).astype(F32)
    return jnp.where(row < 4, high, pltpu.roll(weights - high, 4, axis=0)).astype(BF16)


def pair_other(other, home, row):
    block = other - anchor_of(home, row)
    turned = swapped(block, row)
    norm = split3_wide(over_rows(block * block, row < 3))
    drift = over_rows(block * turned, row < 3)
    drift_high = drift.astype(BF16).astype(F32)
    one = jnp.ones((8, 128), F32)
    end = by_row(row, [norm[0], norm[1], norm[2], drift_high, drift - drift_high, one, one, one])
    part = split3_wide(block)
    left = stacked(
        [part[0], part[0], part[1], part[1], part[0], part[2], end, jnp.zeros((8, 128), F32)]
    ).astype(BF16)
    weights = jnp.where(row < 3, block, 1.0) * jnp.broadcast_to(block[6:7], (8, 128))
    return left, low_below(weights, row)


def wall_home(home, row):
    block = home - AXIS_CENTRE
    norm = split3_wide(-over_rows(block * block, row < 3))
    parts = split3_wide(block)
    zero = jnp.zeros((8, 128), F32)
    high = [jnp.where(row < 3, part, 0.0) for part in parts]
    wide = [
        jnp.where(jnp.logical_and(row >= 3, row < 6), 2.0 * pltpu.roll(part, 3, axis=0), 0.0)
        for part in parts
    ]
    level = jnp.where(row == 7, -1.0, 0.0)
    six = (row == 6).astype(F32)
    end = by_row(row, [norm[0], norm[1], norm[2], zero])
    return jnp.concatenate(
        [
            stacked([high[0] + level, high[1], high[0] + level, high[1], high[2], high[0] + level, zero, zero]),
            stacked([wide[0] + six, wide[1], wide[0] + six, wide[1], wide[2], wide[0] + six, end, zero]),
        ],
        axis=1,
    ).astype(BF16)


def wall_other(blades, row):
    part = split3_wide(blades)
    end = jnp.where(row < 3, 1.0, 0.0)
    left = stacked(
        [part[0], part[0], part[1], part[1], part[0], part[2], end, jnp.zeros((8, 128), F32)]
    ).astype(BF16)
    reach = over_rows(blades * blades, jnp.logical_and(row >= 3, row < 6))
    weights = blades / (reach + jnp.broadcast_to(blades[6:7], (8, 128)))
    return left, low_below(weights, row)


def weighted(weights, strength):
    high, low = split2(strength)
    return jnp.dot(
        jnp.concatenate([weights, weights], axis=1),
        jnp.concatenate([high, low], axis=0),
        preferred_element_type=F32,
    )


def kernel(
    pos_h, vel_h, rad_h, vert_h, speed_h, order_h, angles, ghost_ids, home_ids, other_ids,
    wall_ids, wall_picks, counts,
    pos_o, vel_o, rad_o,
    bodies, corners, speeds, order, own, pool_0, pool_1, pool_2, lent, tri_0, tri_1, tri_2,
    outgoing, arrived, lane_hot, block_hot,
    pair_sel, wall_sel, pair_out, wall_out,
    pair_right, pair_left, pair_weight, wall_right, wall_left, wall_weight,
    in_sem, ghost_send, ghost_recv, mig_send, mig_recv,
    zh_send, zh_recv, x_send, x_recv, xz_send, xz_recv, core_send, core_recv,
):
    pool, tri = (pool_0, pool_1, pool_2), (tri_0, tri_1, tri_2)
    gx = lax.axis_index("gx")
    gy = lax.axis_index("gy")
    gz = lax.axis_index("gz")
    me = gy * 4 + gz
    x_at, zh, core = gx // 4, (gx // 2) % 2, gx % 2
    twin = gx + 1 - 2 * core
    zmate = gx + 2 - 4 * zh

    loads = [
        pltpu.make_async_copy(vert_h, corners, in_sem.at[0]),
        pltpu.make_async_copy(speed_h, speeds, in_sem.at[1]),
        pltpu.make_async_copy(pos_h, bodies.at[pl.ds(0, 3)], in_sem.at[2]),
        pltpu.make_async_copy(vel_h, bodies.at[pl.ds(3, 3)], in_sem.at[3]),
        pltpu.make_async_copy(rad_h, bodies.at[6], in_sem.at[4]),
        pltpu.make_async_copy(order_h.at[:, pl.ds(0, 8), :], order, in_sem.at[5]),
    ]
    for load in loads:
        load.start()

    def peer_of(hop):
        row, column = lax.rem(gy + hop // 4, 4), lax.rem(gz + hop % 4, 4)
        return row * 4 + column, (gx, row, column)

    def x_mate(hop, z_of):
        index = lax.rem(x_at + hop, 4) * 4 + z_of * 2 + core
        return index

    faces = [
        (gx > 0, gx < SLABS - 1, (gx + 1, gy, gz)),
        (gx < SLABS - 1, gx > 0, (gx - 1, gy, gz)),
        (gy > 0, gy < 3, (gx, gy + 1, gz)),
        (gy < 3, gy > 0, (gx, gy - 1, gz)),
        (gz > 0, gz < 3, (gx, gy, gz + 1)),
        (gz < 3, gz > 0, (gx, gy, gz - 1)),
    ]

    barrier = pltpu.get_barrier_semaphore()

    def greet(hop, carry):
        pl.semaphore_signal(barrier, inc=1, device_id=peer_of(hop)[1], device_id_type=MESH)
        return carry

    lax.fori_loop(1, GROUP, greet, 0)
    for other in (twin, zmate, x_mate(1, zh), x_mate(2, zh), x_mate(3, zh)):
        pl.semaphore_signal(barrier, inc=1, device_id=(other, gy, gz), device_id_type=MESH)
    for _, borrower, target in faces[:2]:
        @pl.when(borrower)
        def _():
            pl.semaphore_signal(barrier, inc=1, device_id=target, device_id_type=MESH)

    def ghost_copy(step, face, target):
        return pltpu.make_async_remote_copy(
            src_ref=lent.at[step],
            dst_ref=pool[step].at[pl.ds(NBLK + GHOST * face, GHOST)],
            send_sem=ghost_send.at[step, face],
            recv_sem=ghost_recv.at[step, face],
            device_id=target,
            device_id_type=MESH,
        )

    def tri_copy(step, owner, target, send, recv):
        part = tri[step].at[pl.ds(owner * TRIBLK, TRIBLK)]
        return pltpu.make_async_remote_copy(
            src_ref=part,
            dst_ref=part,
            send_sem=send,
            recv_sem=recv,
            device_id=(target, gy, gz),
            device_id_type=MESH,
        )

    def zh_copy(step):
        return tri_copy(step, gx, zmate, zh_send.at[step], zh_recv.at[step])

    def core_copy(step, owner, slot):
        return tri_copy(step, owner, twin, core_send.at[step, slot], core_recv.at[step, slot])

    def x_copy(step, hop):
        return tri_copy(step, gx, x_mate(hop, zh), x_send.at[step, hop - 1], x_recv.at[step, hop - 1])

    def xz_copy(step, hop):
        return tri_copy(step, zmate, x_mate(hop, zh), xz_send.at[step, hop - 1], xz_recv.at[step, hop - 1])

    def mig_copy(step, hop):
        peer, target = peer_of(hop)
        return pltpu.make_async_remote_copy(
            src_ref=outgoing.at[step, peer // 8],
            dst_ref=arrived.at[step, me],
            send_sem=mig_send.at[step, hop],
            recv_sem=mig_recv.at[step, hop],
            device_id=target,
            device_id_type=MESH,
        )

    def lend(step):
        for row in range(7):
            own[:, row, :] = bodies[row]
        own[:, 7, :] = jnp.zeros((NBLK, 128), F32)
        for slot in range(GHOST):
            lent[step, slot] = own[ghost_ids[slot]]

    def send_ghosts(step):
        for face, (_, borrower, target) in enumerate(faces):
            @pl.when(borrower)
            def _():
                ghost_copy(step, face, target).start()
        pool[step][pl.ds(0, NBLK)] = own[...]

    def wait_ghosts(step):
        for face, (lender, _, target) in enumerate(faces):
            @pl.when(lender)
            def _():
                ghost_copy(step, face, target).wait_recv()

    def blade_move(step):
        angle = jnp.full((8, 128), angles[step], F32)
        cosine = jnp.cos(angle)[0:1]
        sine = jnp.sin(angle)[0:1]
        now = []
        for corner in range(3):
            along = corners[3 * corner]
            rel_y = corners[3 * corner + 1] - AXIS_CENTRE
            rel_z = corners[3 * corner + 2] - AXIS_CENTRE
            for j, value in enumerate((
                along,
                AXIS_CENTRE + cosine * rel_y - sine * rel_z,
                AXIS_CENTRE + sine * rel_y + cosine * rel_z,
            )):
                moved = value + TIME_STEP * speeds[3 * corner + j]
                corners[3 * corner + j] = moved
                now.append(moved)
        a, b, c = now[0:3], now[3:6], now[6:9]
        centre = [(a[i] + b[i] + c[i]) / 3.0 for i in range(3)]
        u = [b[i] - a[i] for i in range(3)]
        w = [c[i] - a[i] for i in range(3)]
        area = [
            u[1] * w[2] - u[2] * w[1],
            u[2] * w[0] - u[0] * w[2],
            u[0] * w[1] - u[1] * w[0],
        ]
        length = jnp.sqrt(area[0] * area[0] + area[1] * area[1] + area[2] * area[2])
        scale = 1.0 / jnp.maximum(length, AREA_FLOOR)
        normal = [area[i] * scale for i in range(3)]
        spread = SPREAD_PAD
        for corner in (a, b, c):
            for i in range(3):
                spread = spread + (corner[i] - centre[i]) ** 2 * (1.0 / 3.0)
        shifted = [centre[i] - AXIS_CENTRE for i in range(3)]
        square = shifted[0] ** 2 + shifted[1] ** 2 + shifted[2] ** 2
        level = normal[0] * shifted[0] + normal[1] * shifted[1] + normal[2] * shifted[2]
        rows = normal + shifted + [spread - square, level]
        for row in range(8):
            tri[step][pl.ds(gx * TRIBLK, TRIBLK), row, :] = rows[row]

    def start_tri(step):
        core_copy(step, gx, 0).start()
        for hop in (1, 2, 3):
            x_copy(step, hop).start()

    def forward_tri(step):
        zh_copy(step).wait_recv()
        for hop in (1, 2, 3):
            xz_copy(step, hop).start()
        core_copy(step, zmate, 1).start()

    def pass_near(step):
        for hop in (1, 2, 3):
            x_copy(step, hop).wait_recv()
            core_copy(step, x_mate(4 - hop, zh), 1 + hop).start()

    def pass_far(step):
        for hop in (1, 2, 3):
            xz_copy(step, hop).wait_recv()
            core_copy(step, x_mate(4 - hop, 1 - zh), 4 + hop).start()

    def wait_tri(step):
        for slot in range(8):
            core_copy(step, gx, slot).wait_recv()

    def prepare():
        lane = lax.broadcasted_iota(jnp.int32, (128, 256), 0)
        block = lax.broadcasted_iota(jnp.int32, (NBLK, 256), 0)
        place = lax.broadcasted_iota(jnp.int32, (1, 256), 1)
        for step in range(STEPS):
            ids = jnp.concatenate([order[step, 0:1, :], order[step, 1:2, :]], axis=1)
            lane_hot[step] = (jnp.bitwise_and(ids, 127) == lane).astype(F32).astype(BF16)
            limit = jnp.zeros((1, 256), jnp.int32)
            for peer in range(GROUP):
                limit = jnp.where(lax.shift_right_logical(place, 4) == peer, counts[step, 0, peer], limit)
            filled = jnp.bitwise_and(place, 15) < limit
            hot = lax.shift_right_logical(ids, 7) == block
            block_hot[step, 0] = hot.astype(F32)
            block_hot[step, 1] = jnp.logical_and(hot, filled).astype(F32)
        home = lax.broadcasted_iota(jnp.int32, (1, 128), 1)
        hot = [(home == home_ids[tile]).astype(F32) for tile in range(TILES)]
        pair_sel[...] = stacked(hot).T[0:NBLK].astype(BF16)
        hot = [(home == wall_ids[tile]).astype(F32) for tile in range(TTILES)]
        wall_sel[...] = stacked(hot).T[0:NBLK].astype(BF16)

    def pair_homes():
        def some(turn, carry):
            row = lax.broadcasted_iota(jnp.int32, (8, 128), 0)
            for spot in range(SOME):
                tile = turn * SOME + spot
                pair_right[tile] = pair_home(own[home_ids[tile]], row)
            return carry

        lax.fori_loop(0, TILES // SOME, some, 0)

    def pair_features(step):
        def features(turn, carry):
            row = lax.broadcasted_iota(jnp.int32, (8, 128), 0)
            for spot in range(SOME):
                tile = turn * SOME + spot
                left, weights = pair_other(pool[step][other_ids[tile]], own[home_ids[tile]], row)
                pair_left[tile] = left.T
                pair_weight[tile] = weights
            return carry

        lax.fori_loop(0, TILES // SOME, features, 0)

    def pair_forces(first, last):
        def forces(turn, carry):
            tiles = [turn * SOME + spot for spot in range(SOME)]
            forms = [
                jnp.dot(pair_left[tile], pair_right[tile], preferred_element_type=F32)
                for tile in tiles
            ]
            strengths = []
            for form in forms:
                square = jnp.maximum(form[:, 0:128], SOFTENING)
                speed, reach = form[:, 128:256], form[:, 256:384]
                scaled = square * reach
                ratio = lax.rsqrt(scaled * reach)
                overlap = jnp.maximum(reach - scaled * ratio, 0.0)
                strengths.append(overlap * ratio * (STIFFNESS + speed * (reach * ratio)))
            for tile, strength in zip(tiles, strengths):
                pair_out[tile] = weighted(pair_weight[tile], strength)
            return carry

        lax.fori_loop(first, last, forces, 0)

    def wall_homes():
        def some(turn, carry):
            row = lax.broadcasted_iota(jnp.int32, (8, 128), 0)
            for spot in range(SOME):
                tile = turn * SOME + spot
                wall_right[tile] = wall_home(own[wall_ids[tile]], row)
            return carry

        lax.fori_loop(0, TTILES // SOME, some, 0)

    def wall_features(step):
        def features(turn, carry):
            row = lax.broadcasted_iota(jnp.int32, (8, 128), 0)
            for spot in range(SOME):
                tile = turn * SOME + spot
                left, weights = wall_other(tri[step][wall_picks[tile]], row)
                wall_left[tile] = left.T
                wall_weight[tile] = weights
            return carry

        lax.fori_loop(0, TTILES // SOME, features, 0)

    def wall_forces():
        def forces(turn, carry):
            tiles = [turn * SOME + spot for spot in range(SOME)]
            forms = [
                jnp.dot(wall_left[tile], wall_right[tile], preferred_element_type=F32)
                for tile in tiles
            ]
            strengths = []
            for tile, form in zip(tiles, forms):
                radius = own[wall_ids[tile]][6:7, :]
                height, window = form[:, 0:128], form[:, 128:256]
                depth = jnp.maximum(radius - jnp.abs(height), 0.0)
                strengths.append(depth * height * jnp.maximum(window, 0.0))
            for tile, strength in zip(tiles, strengths):
                wall_out[tile] = weighted(wall_weight[tile], strength)
            return carry

        lax.fori_loop(0, TTILES // SOME, forces, 0)

    def integrate():
        def home_sum(select, out, row):
            high, low = split2(out[:, row, :] + out[:, row + 4, :])
            return jnp.dot(select, high, preferred_element_type=F32) + jnp.dot(
                select, low, preferred_element_type=F32
            )

        pairs, walls = pair_sel[...], wall_sel[...]
        weight = home_sum(pairs, pair_out, 3)
        radius = bodies[6]
        inertia = 1.0 / (radius * radius)
        for i in range(3):
            place = bodies[i]
            contact = (place - place[:, 0:1]) * weight - home_sum(pairs, pair_out, i)
            pull = (contact + WALL_STIFF * home_sum(walls, wall_out, i)) * inertia
            if i == 2:
                pull = pull - GRAVITY
            velocity = bodies[3 + i] + TIME_STEP * pull
            bodies[3 + i] = velocity
            bodies[i] = place + TIME_STEP * velocity

    def send_migrants(step):
        hot = lane_hot[step]
        parts = split3(bodies[...].reshape(7 * NBLK, 128))
        picked = jnp.dot(parts[0], hot, preferred_element_type=F32)
        picked = picked + jnp.dot(parts[1], hot, preferred_element_type=F32)
        picked = picked + jnp.dot(parts[2], hot, preferred_element_type=F32)
        hit = block_hot[step, 0] > 0.5
        for row in range(7):
            line = jnp.where(hit, picked[NBLK * row : NBLK * row + NBLK], 0.0)
            line = jnp.sum(line, axis=0, keepdims=True)
            outgoing[step, 0, row : row + 1, :] = line[:, 0:128]
            outgoing[step, 1, row : row + 1, :] = line[:, 128:256]
        for half in range(2):
            outgoing[step, half, 7:8, :] = jnp.zeros((1, 128), F32)

        for along in (2, 1, 3, 0):
            for across in (1, 3, 2, 0):
                if along or across:
                    mig_copy(step, 4 * across + along).start()

    def take_migrants(step):
        def wait(hop, carry):
            mig_copy(step, hop).wait_recv()
            return carry

        lax.fori_loop(1, GROUP, wait, 0)
        place = lax.shift_right_logical(lax.broadcasted_iota(jnp.int32, (8, 128), 1), 4)
        shift = (me % 8) * 16
        halves = []
        for half in range(2):
            whole = jnp.zeros((8, 128), F32)
            for spot in range(8):
                turned = pltpu.roll(
                    arrived[step, 8 * half + spot], lax.rem(16 * spot + 128 - shift, 128), axis=1
                )
                whole = jnp.where(place == spot, turned, whole)
            halves.append(whole)
        values = jnp.concatenate(halves, axis=1)
        filled = block_hot[step, 1] > 0.5
        spread = jnp.concatenate(
            [jnp.where(filled, values[row : row + 1, :], 0.0) for row in range(7)], axis=0
        )
        dims = (((1,), (1,)), ((), ()))
        hot = lane_hot[step]
        landed = jnp.zeros((7 * NBLK, 128), F32)
        for part in split3(spread):
            landed = landed + lax.dot_general(part, hot, dims, preferred_element_type=F32)
        hits = lax.dot_general(
            block_hot[step, 1].astype(BF16), hot, dims, preferred_element_type=F32
        )
        for row in range(7):
            bodies[row] = jnp.where(hits > 0.5, landed[NBLK * row : NBLK * row + NBLK], bodies[row])

    for step in range(STEPS):
        for face, (lender, _, _) in enumerate(faces):
            @pl.when(jnp.logical_not(lender))
            def _():
                pool[step][pl.ds(NBLK + GHOST * face, GHOST)] = jnp.zeros((GHOST, 8, 128), F32)
        arrived[step, me] = jnp.zeros((8, 128), F32)

    for load in loads:
        load.wait()
    lend(0)
    blade_move(0)
    neighbours = 20 + (gx > 0).astype(jnp.int32) + (gx < SLABS - 1).astype(jnp.int32)
    pl.semaphore_wait(barrier, neighbours)

    for step in range(STEPS):
        if step == 0:
            zh_copy(0).start()
        else:
            lend(step)
        send_ghosts(step)
        if step == 0:
            start_tri(0)
            pair_homes()
            blade_move(1)
            pass_near(0)
            forward_tri(0)
            blade_move(2)
            wall_homes()
            prepare()
            wait_ghosts(0)
            pair_features(0)
            pair_forces(0, 1)
            pass_far(0)
            zh_copy(1).start()
            start_tri(1)
            pair_forces(1, 2)
            wait_tri(0)
            wall_features(0)
            wall_forces()
        else:
            wall_homes()
            pair_homes()
            pass_far(step)
            if step == 1:
                forward_tri(2)
                pass_near(2)
            wait_tri(step)
            wall_features(step)
            wall_forces()
            wait_ghosts(step)
            pair_features(step)
            pair_forces(0, 2)
        integrate()
        send_migrants(step)
        if step == 0:
            pass_near(1)
            forward_tri(1)
            zh_copy(2).start()
            start_tri(2)
        take_migrants(step)

    pos_o[...] = bodies[0:3]
    vel_o[...] = bodies[3:6]
    rad_o[...] = bodies[6]
    for step in range(STEPS):
        for face, (_, borrower, target) in enumerate(faces):
            @pl.when(borrower)
            def _():
                ghost_copy(step, face, target).wait_send()
        zh_copy(step).wait_send()
        for hop in (1, 2, 3):
            x_copy(step, hop).wait_send()
            xz_copy(step, hop).wait_send()
        for slot in range(8):
            core_copy(step, gx, slot).wait_send()

        def wait(hop, carry):
            mig_copy(step, hop).wait_send()
            return carry

        lax.fori_loop(1, GROUP, wait, 0)


def shards(
    position, velocity, radius, vertices, vertex_speed, angles, ghost_blocks,
    tile_home, tile_other, wall_home, wall_block, mig_order, mig_count,
):
    whole = pl.BlockSpec(memory_space=pl.ANY)
    scalars = pl.BlockSpec(memory_space=pltpu.SMEM)
    here = pl.BlockSpec(memory_space=pltpu.VMEM)
    dma = pltpu.SemaphoreType.DMA
    out = pl.pallas_call(
        kernel,
        out_shape=(
            pltpu.VMEM((3, NBLK, 128), F32),
            pltpu.VMEM((3, NBLK, 128), F32),
            pltpu.VMEM((NBLK, 128), F32),
        ),
        in_specs=[whole] * 6 + [scalars] * 7,
        out_specs=(here, here, here),
        scratch_shapes=[
            pltpu.VMEM((7, NBLK, 128), F32),
            pltpu.VMEM((9, TRIBLK, 128), F32),
            pltpu.VMEM((9, TRIBLK, 128), F32),
            pltpu.VMEM((STEPS, 8, 128), jnp.int32),
            pltpu.VMEM((NBLK, 8, 128), F32),
            *[pltpu.VMEM((POOL, 8, 128), F32) for _ in range(STEPS)],
            pltpu.VMEM((STEPS, GHOST, 8, 128), F32),
            *[pltpu.VMEM((SLABS * TRIBLK, 8, 128), F32) for _ in range(STEPS)],
            pltpu.VMEM((STEPS, 2, 8, 128), F32),
            pltpu.VMEM((STEPS, GROUP, 8, 128), F32),
            pltpu.VMEM((STEPS, 128, 256), BF16),
            pltpu.VMEM((STEPS, 2, NBLK, 256), F32),
            pltpu.VMEM((NBLK, TILES), BF16),
            pltpu.VMEM((NBLK, TTILES), BF16),
            pltpu.VMEM((TILES, 8, 128), F32),
            pltpu.VMEM((TTILES, 8, 128), F32),
            pltpu.VMEM((TILES, 64, 384), BF16),
            pltpu.VMEM((TILES, 128, 64), BF16),
            pltpu.VMEM((TILES, 8, 128), BF16),
            pltpu.VMEM((TTILES, 64, 256), BF16),
            pltpu.VMEM((TTILES, 128, 64), BF16),
            pltpu.VMEM((TTILES, 8, 128), BF16),
            dma((6,)),
            dma((STEPS, 6)),
            dma((STEPS, 6)),
            dma((STEPS, GROUP)),
            dma((STEPS, GROUP)),
            dma((STEPS,)),
            dma((STEPS,)),
            dma((STEPS, 3)),
            dma((STEPS, 3)),
            dma((STEPS, 3)),
            dma((STEPS, 3)),
            dma((STEPS, 8)),
            dma((STEPS, 8)),
        ],
        compiler_params=pltpu.CompilerParams(
            collective_id=0, has_side_effects=True, vmem_limit_bytes=60 * 1024 * 1024
        ),
    )(
        position.reshape(3, NBLK, 128),
        velocity.reshape(3, NBLK, 128),
        radius.reshape(NBLK, 128),
        vertices.reshape(9, TRIBLK, 128),
        vertex_speed.reshape(9, TRIBLK, 128),
        mig_order.reshape(STEPS, NBLK, 128),
        angles,
        ghost_blocks.reshape(-1),
        tile_home.reshape(-1),
        tile_other.reshape(-1),
        wall_home.reshape(-1),
        wall_block.reshape(-1),
        mig_count.reshape(STEPS, 1, GROUP),
    )
    return (
        out[0].reshape(position.shape),
        out[1].reshape(velocity.shape),
        out[2].reshape(radius.shape),
    )


def solution(mesh):
    block = P("gx", "gy", "gz", None)
    blocks = P(None, "gx", "gy", "gz", None)
    in_specs = (
        blocks, blocks, block, blocks, blocks, P(), block, block, block, block, block, blocks, blocks,
    )
    return jax.shard_map(
        shards, mesh=mesh, in_specs=in_specs, out_specs=(blocks, blocks, block), check_vma=False
    )
```

```python
import functools

import jax
import jax.numpy as jnp
from jax import lax
from jax.experimental import pallas as pl
from jax.experimental.pallas import tpu as pltpu
from jax.sharding import PartitionSpec as P

MESH = pl.DeviceIdType.MESH
F32 = jnp.float32
BF16 = jnp.bfloat16

STEPS = 3
NBLK = 32
GHOST = 16
POOL = 128
TILES = 64
TTILES = 32
TRIBLK = 16
SLABS = 16
GROUP = 16
MC = 16
SOME = 32
SOON = 8

STIFFNESS = 20.0
DAMPING = 2.0
WALL_STIFF = 20.0
SOFTENING = 0.01
TIME_STEP = 0.02
GRAVITY = 1.0
AXIS_CENTRE = 2.0
AREA_FLOOR = 1.0
SPREAD_PAD = 0.25


def split3(values):
    high = values.astype(BF16)
    rest = values - high.astype(F32)
    middle = rest.astype(BF16)
    low = (rest - middle.astype(F32)).astype(BF16)
    return high, middle, low


def split2(values):
    high = values.astype(BF16)
    low = (values - high.astype(F32)).astype(BF16)
    return high, low


def split3_wide(values):
    high = values.astype(BF16).astype(F32)
    rest = values - high
    middle = rest.astype(BF16).astype(F32)
    return high, middle, rest - middle


def swapped(block, row):
    return jnp.where(row < 3, pltpu.roll(block, 5, axis=0), pltpu.roll(block, 3, axis=0))


def over_rows(values, mask):
    total = jnp.sum(jnp.where(mask, values, 0.0), axis=0, keepdims=True)
    return jnp.broadcast_to(total, (8, 128))


def by_row(row, values):
    out = values[-1]
    for i in range(len(values) - 2, -1, -1):
        out = jnp.where(row == i, values[i], out)
    return out


def stacked(groups):
    return jnp.concatenate(groups, axis=0)


def anchor_of(home, row):
    return jnp.where(row < 6, jnp.broadcast_to(home[:, 0:1], (8, 128)), 0.0)


def pair_home(home, row):
    block = home - anchor_of(home, row)
    turned = swapped(block, row)
    norm = split3_wide(over_rows(block * block, row < 3) + SOFTENING)
    drift = split3_wide(-DAMPING * over_rows(block * turned, row < 3))
    size = split3_wide(jnp.broadcast_to(block[6:7], (8, 128)))
    zero, one = jnp.zeros((8, 128), F32), jnp.ones((8, 128), F32)
    near = [jnp.where(row < 3, -2.0 * part, 0.0) for part in split3_wide(block)]
    cross = [jnp.where(row < 6, DAMPING * part, 0.0) for part in split3_wide(turned)]
    six = (row == 6).astype(F32)
    near_end = by_row(row, [one, one, one, zero, zero, norm[0], norm[1], norm[2]])
    cross_end = by_row(
        row, [zero, zero, zero, -DAMPING * one, -DAMPING * one, drift[0], drift[1], drift[2]]
    )
    size_end = by_row(row, [zero, zero, zero, zero, zero, size[0], size[1], size[2]])
    return jnp.concatenate(
        [
            stacked([near[0], near[1], near[0], near[1], near[2], near[0], near_end, zero]),
            stacked([cross[0], cross[1], cross[0], cross[1], cross[2], cross[0], cross_end, zero]),
            stacked([six, zero, six, zero, zero, six, size_end, zero]),
        ],
        axis=1,
    ).astype(BF16)


def low_below(weights, row):
    high = weights.astype(BF16).astype(F32)
    return jnp.where(row < 4, high, pltpu.roll(weights - high, 4, axis=0)).astype(BF16)


def pair_other(other, home, row):
    block = other - anchor_of(home, row)
    turned = swapped(block, row)
    norm = split3_wide(over_rows(block * block, row < 3))
    drift = over_rows(block * turned, row < 3)
    drift_high = drift.astype(BF16).astype(F32)
    one = jnp.ones((8, 128), F32)
    end = by_row(row, [norm[0], norm[1], norm[2], drift_high, drift - drift_high, one, one, one])
    part = split3_wide(block)
    left = stacked(
        [part[0], part[0], part[1], part[1], part[0], part[2], end, jnp.zeros((8, 128), F32)]
    ).astype(BF16)
    weights = jnp.where(row < 3, block, 1.0) * jnp.broadcast_to(block[6:7], (8, 128))
    return left, low_below(weights, row)


def wall_home(home, row):
    block = home - AXIS_CENTRE
    norm = split3_wide(-over_rows(block * block, row < 3))
    parts = split3_wide(block)
    zero = jnp.zeros((8, 128), F32)
    high = [jnp.where(row < 3, part, 0.0) for part in parts]
    wide = [
        jnp.where(jnp.logical_and(row >= 3, row < 6), 2.0 * pltpu.roll(part, 3, axis=0), 0.0)
        for part in parts
    ]
    level = jnp.where(row == 7, -1.0, 0.0)
    six = (row == 6).astype(F32)
    end = by_row(row, [norm[0], norm[1], norm[2], zero])
    return jnp.concatenate(
        [
            stacked([high[0] + level, high[1], high[0] + level, high[1], high[2], high[0] + level, zero, zero]),
            stacked([wide[0] + six, wide[1], wide[0] + six, wide[1], wide[2], wide[0] + six, end, zero]),
        ],
        axis=1,
    ).astype(BF16)


def wall_other(blades, row):
    part = split3_wide(blades)
    end = jnp.where(row < 3, 1.0, 0.0)
    left = stacked(
        [part[0], part[0], part[1], part[1], part[0], part[2], end, jnp.zeros((8, 128), F32)]
    ).astype(BF16)
    reach = over_rows(blades * blades, jnp.logical_and(row >= 3, row < 6))
    weights = blades / (reach + jnp.broadcast_to(blades[6:7], (8, 128)))
    return left, low_below(weights, row)


def weighted(weights, strength):
    high, low = split2(strength)
    return jnp.dot(
        jnp.concatenate([weights, weights], axis=1),
        jnp.concatenate([high, low], axis=0),
        preferred_element_type=F32,
    )


def kernel(
    pos_h, vel_h, rad_h, vert_h, speed_h, order_h, angles, ghost_ids, home_ids, other_ids,
    wall_ids, wall_picks, counts,
    pos_o, vel_o, rad_o,
    bodies, corners, speeds, order, own, pool_0, pool_1, pool_2, lent, tri_0, tri_1, tri_2,
    outgoing, arrived, lane_hot, block_hot,
    pair_sel, wall_sel, pair_out, wall_out,
    pair_right, wall_right, wall_left, wall_weight,
    in_sem, ghost_send, ghost_recv, mig_send, mig_recv,
    zh_send, zh_recv, x_send, x_recv, xz_send, xz_recv, core_send, core_recv,
):
    pool, tri = (pool_0, pool_1, pool_2), (tri_0, tri_1, tri_2)
    gx = lax.axis_index("gx")
    gy = lax.axis_index("gy")
    gz = lax.axis_index("gz")
    me = gy * 4 + gz
    x_at, zh, core = gx // 4, (gx // 2) % 2, gx % 2
    twin = gx + 1 - 2 * core
    zmate = gx + 2 - 4 * zh

    loads = [
        pltpu.make_async_copy(vert_h, corners, in_sem.at[0]),
        pltpu.make_async_copy(speed_h, speeds, in_sem.at[1]),
        pltpu.make_async_copy(pos_h, bodies.at[pl.ds(0, 3)], in_sem.at[2]),
        pltpu.make_async_copy(vel_h, bodies.at[pl.ds(3, 3)], in_sem.at[3]),
        pltpu.make_async_copy(rad_h, bodies.at[6], in_sem.at[4]),
        pltpu.make_async_copy(order_h.at[:, pl.ds(0, 8), :], order, in_sem.at[5]),
    ]
    for load in loads:
        load.start()

    def peer_of(hop):
        row, column = lax.rem(gy + hop // 4, 4), lax.rem(gz + hop % 4, 4)
        return row * 4 + column, (gx, row, column)

    def x_mate(hop, z_of):
        index = lax.rem(x_at + hop, 4) * 4 + z_of * 2 + core
        return index

    faces = [
        (gx > 0, gx < SLABS - 1, (gx + 1, gy, gz)),
        (gx < SLABS - 1, gx > 0, (gx - 1, gy, gz)),
        (gy > 0, gy < 3, (gx, gy + 1, gz)),
        (gy < 3, gy > 0, (gx, gy - 1, gz)),
        (gz > 0, gz < 3, (gx, gy, gz + 1)),
        (gz < 3, gz > 0, (gx, gy, gz - 1)),
    ]

    barrier = pltpu.get_barrier_semaphore()

    def greet(hop, carry):
        pl.semaphore_signal(barrier, inc=1, device_id=peer_of(hop)[1], device_id_type=MESH)
        return carry

    lax.fori_loop(1, GROUP, greet, 0)
    for other in (twin, zmate, x_mate(1, zh), x_mate(2, zh), x_mate(3, zh)):
        pl.semaphore_signal(barrier, inc=1, device_id=(other, gy, gz), device_id_type=MESH)
    for _, borrower, target in faces[:2]:
        @pl.when(borrower)
        def _():
            pl.semaphore_signal(barrier, inc=1, device_id=target, device_id_type=MESH)

    def ghost_copy(step, face, target):
        return pltpu.make_async_remote_copy(
            src_ref=lent.at[step],
            dst_ref=pool[step].at[pl.ds(NBLK + GHOST * face, GHOST)],
            send_sem=ghost_send.at[step, face],
            recv_sem=ghost_recv.at[step, face],
            device_id=target,
            device_id_type=MESH,
        )

    def tri_copy(step, owner, target, send, recv):
        part = tri[step].at[pl.ds(owner * TRIBLK, TRIBLK)]
        return pltpu.make_async_remote_copy(
            src_ref=part,
            dst_ref=part,
            send_sem=send,
            recv_sem=recv,
            device_id=(target, gy, gz),
            device_id_type=MESH,
        )

    def zh_copy(step):
        return tri_copy(step, gx, zmate, zh_send.at[step], zh_recv.at[step])

    def core_copy(step, owner, slot):
        return tri_copy(step, owner, twin, core_send.at[step, slot], core_recv.at[step, slot])

    def x_copy(step, hop):
        return tri_copy(step, gx, x_mate(hop, zh), x_send.at[step, hop - 1], x_recv.at[step, hop - 1])

    def xz_copy(step, hop):
        return tri_copy(step, zmate, x_mate(hop, zh), xz_send.at[step, hop - 1], xz_recv.at[step, hop - 1])

    def mig_copy(step, hop):
        peer, target = peer_of(hop)
        return pltpu.make_async_remote_copy(
            src_ref=outgoing.at[step, peer // 8],
            dst_ref=arrived.at[step, me],
            send_sem=mig_send.at[step, hop],
            recv_sem=mig_recv.at[step, hop],
            device_id=target,
            device_id_type=MESH,
        )

    def lend(step):
        for row in range(7):
            own[:, row, :] = bodies[row]
        own[:, 7, :] = jnp.zeros((NBLK, 128), F32)
        for slot in range(GHOST):
            lent[step, slot] = own[ghost_ids[slot]]

    def send_ghosts(step):
        for face, (_, borrower, target) in enumerate(faces):
            @pl.when(borrower)
            def _():
                ghost_copy(step, face, target).start()
        pool[step][pl.ds(0, NBLK)] = own[...]

    def wait_ghosts(step):
        for face, (lender, _, target) in enumerate(faces):
            @pl.when(lender)
            def _():
                ghost_copy(step, face, target).wait_recv()

    def blade_move(step):
        angle = jnp.full((8, 128), angles[step], F32)
        cosine = jnp.cos(angle)[0:1]
        sine = jnp.sin(angle)[0:1]
        now = []
        for corner in range(3):
            along = corners[3 * corner]
            rel_y = corners[3 * corner + 1] - AXIS_CENTRE
            rel_z = corners[3 * corner + 2] - AXIS_CENTRE
            for j, value in enumerate((
                along,
                AXIS_CENTRE + cosine * rel_y - sine * rel_z,
                AXIS_CENTRE + sine * rel_y + cosine * rel_z,
            )):
                moved = value + TIME_STEP * speeds[3 * corner + j]
                corners[3 * corner + j] = moved
                now.append(moved)
        a, b, c = now[0:3], now[3:6], now[6:9]
        centre = [(a[i] + b[i] + c[i]) / 3.0 for i in range(3)]
        u = [b[i] - a[i] for i in range(3)]
        w = [c[i] - a[i] for i in range(3)]
        area = [
            u[1] * w[2] - u[2] * w[1],
            u[2] * w[0] - u[0] * w[2],
            u[0] * w[1] - u[1] * w[0],
        ]
        length = jnp.sqrt(area[0] * area[0] + area[1] * area[1] + area[2] * area[2])
        scale = 1.0 / jnp.maximum(length, AREA_FLOOR)
        normal = [area[i] * scale for i in range(3)]
        spread = SPREAD_PAD
        for corner in (a, b, c):
            for i in range(3):
                spread = spread + (corner[i] - centre[i]) ** 2 * (1.0 / 3.0)
        shifted = [centre[i] - AXIS_CENTRE for i in range(3)]
        square = shifted[0] ** 2 + shifted[1] ** 2 + shifted[2] ** 2
        level = normal[0] * shifted[0] + normal[1] * shifted[1] + normal[2] * shifted[2]
        rows = normal + shifted + [spread - square, level]
        for row in range(8):
            tri[step][pl.ds(gx * TRIBLK, TRIBLK), row, :] = rows[row]

    def start_tri(step):
        core_copy(step, gx, 0).start()
        for hop in (1, 2, 3):
            x_copy(step, hop).start()

    def forward_tri(step):
        zh_copy(step).wait_recv()
        for hop in (1, 2, 3):
            xz_copy(step, hop).start()
        core_copy(step, zmate, 1).start()

    def pass_near(step):
        for hop in (1, 2, 3):
            x_copy(step, hop).wait_recv()
            core_copy(step, x_mate(4 - hop, zh), 1 + hop).start()

    def pass_far(step):
        for hop in (1, 2, 3):
            xz_copy(step, hop).wait_recv()
            core_copy(step, x_mate(4 - hop, 1 - zh), 4 + hop).start()

    def wait_tri(step):
        for slot in range(8):
            core_copy(step, gx, slot).wait_recv()

    def prepare():
        lane = lax.broadcasted_iota(jnp.int32, (128, 256), 0)
        block = lax.broadcasted_iota(jnp.int32, (NBLK, 256), 0)
        place = lax.broadcasted_iota(jnp.int32, (1, 256), 1)
        for step in range(STEPS):
            ids = jnp.concatenate([order[step, 0:1, :], order[step, 1:2, :]], axis=1)
            lane_hot[step] = (jnp.bitwise_and(ids, 127) == lane).astype(F32).astype(BF16)
            limit = jnp.zeros((1, 256), jnp.int32)
            for peer in range(GROUP):
                limit = jnp.where(lax.shift_right_logical(place, 4) == peer, counts[step, 0, peer], limit)
            filled = jnp.bitwise_and(place, 15) < limit
            hot = lax.shift_right_logical(ids, 7) == block
            block_hot[step, 0] = hot.astype(F32)
            block_hot[step, 1] = jnp.logical_and(hot, filled).astype(F32)
        home = lax.broadcasted_iota(jnp.int32, (1, 128), 1)
        hot = [(home == home_ids[tile]).astype(F32) for tile in range(TILES)]
        pair_sel[...] = stacked(hot).T[0:NBLK].astype(BF16)
        hot = [(home == wall_ids[tile]).astype(F32) for tile in range(TTILES)]
        wall_sel[...] = stacked(hot).T[0:NBLK].astype(BF16)

    def pair_homes():
        def some(turn, carry):
            row = lax.broadcasted_iota(jnp.int32, (8, 128), 0)
            for spot in range(SOME):
                tile = turn * SOME + spot
                pair_right[tile] = pair_home(own[home_ids[tile]], row)
            return carry

        lax.fori_loop(0, TILES // SOME, some, 0)

    def pair_forces(step, halfway=None):
        row = lax.broadcasted_iota(jnp.int32, (8, 128), 0)
        ready, formed = {}, {}
        for turn in range(TILES + 2 * SOON):
            if halfway is not None and turn == TILES // 2 + SOON:
                halfway()
            if turn < TILES:
                left, weights = pair_other(
                    pool[step][other_ids[turn]], own[home_ids[turn]], row
                )
                ready[turn] = (left.T, weights)
            tile = turn - SOON
            if 0 <= tile < TILES:
                formed[tile] = jnp.dot(
                    ready[tile][0], pair_right[tile], preferred_element_type=F32
                )
            tile = turn - 2 * SOON
            if tile >= 0:
                form = formed.pop(tile)
                square = jnp.maximum(form[:, 0:128], SOFTENING)
                speed, reach = form[:, 128:256], form[:, 256:384]
                scaled = square * reach
                ratio = lax.rsqrt(scaled * reach)
                overlap = jnp.maximum(reach - scaled * ratio, 0.0)
                strength = overlap * ratio * (STIFFNESS + speed * (reach * ratio))
                pair_out[tile] = weighted(ready.pop(tile)[1], strength)

    def wall_homes():
        def some(turn, carry):
            row = lax.broadcasted_iota(jnp.int32, (8, 128), 0)
            for spot in range(SOME):
                tile = turn * SOME + spot
                wall_right[tile] = wall_home(own[wall_ids[tile]], row)
            return carry

        lax.fori_loop(0, TTILES // SOME, some, 0)

    def wall_features(step):
        def features(turn, carry):
            row = lax.broadcasted_iota(jnp.int32, (8, 128), 0)
            for spot in range(SOME):
                tile = turn * SOME + spot
                left, weights = wall_other(tri[step][wall_picks[tile]], row)
                wall_left[tile] = left.T
                wall_weight[tile] = weights
            return carry

        lax.fori_loop(0, TTILES // SOME, features, 0)

    def wall_forces():
        def forces(turn, carry):
            tiles = [turn * SOME + spot for spot in range(SOME)]
            forms = [
                jnp.dot(wall_left[tile], wall_right[tile], preferred_element_type=F32)
                for tile in tiles
            ]
            strengths = []
            for tile, form in zip(tiles, forms):
                radius = own[wall_ids[tile]][6:7, :]
                height, window = form[:, 0:128], form[:, 128:256]
                depth = jnp.maximum(radius - jnp.abs(height), 0.0)
                strengths.append(depth * height * jnp.maximum(window, 0.0))
            for tile, strength in zip(tiles, strengths):
                wall_out[tile] = weighted(wall_weight[tile], strength)
            return carry

        lax.fori_loop(0, TTILES // SOME, forces, 0)

    def integrate():
        def home_sum(select, out, row):
            high, low = split2(out[:, row, :] + out[:, row + 4, :])
            return jnp.dot(select, high, preferred_element_type=F32) + jnp.dot(
                select, low, preferred_element_type=F32
            )

        pairs, walls = pair_sel[...], wall_sel[...]
        weight = home_sum(pairs, pair_out, 3)
        radius = bodies[6]
        inertia = 1.0 / (radius * radius)
        for i in range(3):
            place = bodies[i]
            contact = (place - place[:, 0:1]) * weight - home_sum(pairs, pair_out, i)
            pull = (contact + WALL_STIFF * home_sum(walls, wall_out, i)) * inertia
            if i == 2:
                pull = pull - GRAVITY
            velocity = bodies[3 + i] + TIME_STEP * pull
            bodies[3 + i] = velocity
            bodies[i] = place + TIME_STEP * velocity

    def send_migrants(step):
        hot = lane_hot[step]
        parts = split3(bodies[...].reshape(7 * NBLK, 128))
        picked = jnp.dot(parts[0], hot, preferred_element_type=F32)
        picked = picked + jnp.dot(parts[1], hot, preferred_element_type=F32)
        picked = picked + jnp.dot(parts[2], hot, preferred_element_type=F32)
        hit = block_hot[step, 0] > 0.5
        for row in range(7):
            line = jnp.where(hit, picked[NBLK * row : NBLK * row + NBLK], 0.0)
            line = jnp.sum(line, axis=0, keepdims=True)
            outgoing[step, 0, row : row + 1, :] = line[:, 0:128]
            outgoing[step, 1, row : row + 1, :] = line[:, 128:256]
        for half in range(2):
            outgoing[step, half, 7:8, :] = jnp.zeros((1, 128), F32)

        for along in (2, 1, 3, 0):
            for across in (1, 3, 2, 0):
                if along or across:
                    mig_copy(step, 4 * across + along).start()

    def take_migrants(step):
        def wait(hop, carry):
            mig_copy(step, hop).wait_recv()
            return carry

        lax.fori_loop(1, GROUP, wait, 0)
        place = lax.shift_right_logical(lax.broadcasted_iota(jnp.int32, (8, 128), 1), 4)
        shift = (me % 8) * 16
        halves = []
        for half in range(2):
            whole = jnp.zeros((8, 128), F32)
            for spot in range(8):
                turned = pltpu.roll(
                    arrived[step, 8 * half + spot], lax.rem(16 * spot + 128 - shift, 128), axis=1
                )
                whole = jnp.where(place == spot, turned, whole)
            halves.append(whole)
        values = jnp.concatenate(halves, axis=1)
        filled = block_hot[step, 1] > 0.5
        spread = jnp.concatenate(
            [jnp.where(filled, values[row : row + 1, :], 0.0) for row in range(7)], axis=0
        )
        dims = (((1,), (1,)), ((), ()))
        hot = lane_hot[step]
        landed = jnp.zeros((7 * NBLK, 128), F32)
        for part in split3(spread):
            landed = landed + lax.dot_general(part, hot, dims, preferred_element_type=F32)
        hits = lax.dot_general(
            block_hot[step, 1].astype(BF16), hot, dims, preferred_element_type=F32
        )
        for row in range(7):
            bodies[row] = jnp.where(hits > 0.5, landed[NBLK * row : NBLK * row + NBLK], bodies[row])

    for step in range(STEPS):
        for face, (lender, _, _) in enumerate(faces):
            @pl.when(jnp.logical_not(lender))
            def _():
                pool[step][pl.ds(NBLK + GHOST * face, GHOST)] = jnp.zeros((GHOST, 8, 128), F32)
        arrived[step, me] = jnp.zeros((8, 128), F32)

    for load in loads:
        load.wait()
    lend(0)
    blade_move(0)
    neighbours = 20 + (gx > 0).astype(jnp.int32) + (gx < SLABS - 1).astype(jnp.int32)
    pl.semaphore_wait(barrier, neighbours)

    for step in range(STEPS):
        if step == 0:
            zh_copy(0).start()
        else:
            lend(step)
        send_ghosts(step)
        if step == 0:
            start_tri(0)
            pair_homes()
            blade_move(1)
            pass_near(0)
            forward_tri(0)
            blade_move(2)
            wall_homes()
            prepare()
            wait_ghosts(0)

            def halfway():
                pass_far(0)
                zh_copy(1).start()
                start_tri(1)

            pair_forces(0, halfway)
            wait_tri(0)
            wall_features(0)
            wall_forces()
        else:
            wall_homes()
            pair_homes()
            pass_far(step)
            wait_tri(step)
            wall_features(step)
            wall_forces()
            wait_ghosts(step)
            if step == 1:
                zh_copy(2).start()
                start_tri(2)
            pair_forces(step)
        integrate()
        send_migrants(step)
        if step < 2:
            pass_near(step + 1)
            forward_tri(step + 1)
        take_migrants(step)

    pos_o[...] = bodies[0:3]
    vel_o[...] = bodies[3:6]
    rad_o[...] = bodies[6]
    for step in range(STEPS):
        for face, (_, borrower, target) in enumerate(faces):
            @pl.when(borrower)
            def _():
                ghost_copy(step, face, target).wait_send()
        zh_copy(step).wait_send()
        for hop in (1, 2, 3):
            x_copy(step, hop).wait_send()
            xz_copy(step, hop).wait_send()
        for slot in range(8):
            core_copy(step, gx, slot).wait_send()

        def wait(hop, carry):
            mig_copy(step, hop).wait_send()
            return carry

        lax.fori_loop(1, GROUP, wait, 0)


def shards(
    position, velocity, radius, vertices, vertex_speed, angles, ghost_blocks,
    tile_home, tile_other, wall_home, wall_block, mig_order, mig_count,
):
    whole = pl.BlockSpec(memory_space=pl.ANY)
    scalars = pl.BlockSpec(memory_space=pltpu.SMEM)
    here = pl.BlockSpec(memory_space=pltpu.VMEM)
    dma = pltpu.SemaphoreType.DMA
    out = pl.pallas_call(
        kernel,
        out_shape=(
            pltpu.VMEM((3, NBLK, 128), F32),
            pltpu.VMEM((3, NBLK, 128), F32),
            pltpu.VMEM((NBLK, 128), F32),
        ),
        in_specs=[whole] * 6 + [scalars] * 7,
        out_specs=(here, here, here),
        scratch_shapes=[
            pltpu.VMEM((7, NBLK, 128), F32),
            pltpu.VMEM((9, TRIBLK, 128), F32),
            pltpu.VMEM((9, TRIBLK, 128), F32),
            pltpu.VMEM((STEPS, 8, 128), jnp.int32),
            pltpu.VMEM((NBLK, 8, 128), F32),
            *[pltpu.VMEM((POOL, 8, 128), F32) for _ in range(STEPS)],
            pltpu.VMEM((STEPS, GHOST, 8, 128), F32),
            *[pltpu.VMEM((SLABS * TRIBLK, 8, 128), F32) for _ in range(STEPS)],
            pltpu.VMEM((STEPS, 2, 8, 128), F32),
            pltpu.VMEM((STEPS, GROUP, 8, 128), F32),
            pltpu.VMEM((STEPS, 128, 256), BF16),
            pltpu.VMEM((STEPS, 2, NBLK, 256), F32),
            pltpu.VMEM((NBLK, TILES), BF16),
            pltpu.VMEM((NBLK, TTILES), BF16),
            pltpu.VMEM((TILES, 8, 128), F32),
            pltpu.VMEM((TTILES, 8, 128), F32),
            pltpu.VMEM((TILES, 64, 384), BF16),
            pltpu.VMEM((TTILES, 64, 256), BF16),
            pltpu.VMEM((TTILES, 128, 64), BF16),
            pltpu.VMEM((TTILES, 8, 128), BF16),
            dma((6,)),
            dma((STEPS, 6)),
            dma((STEPS, 6)),
            dma((STEPS, GROUP)),
            dma((STEPS, GROUP)),
            dma((STEPS,)),
            dma((STEPS,)),
            dma((STEPS, 3)),
            dma((STEPS, 3)),
            dma((STEPS, 3)),
            dma((STEPS, 3)),
            dma((STEPS, 8)),
            dma((STEPS, 8)),
        ],
        compiler_params=pltpu.CompilerParams(
            collective_id=0, has_side_effects=True, vmem_limit_bytes=60 * 1024 * 1024
        ),
    )(
        position.reshape(3, NBLK, 128),
        velocity.reshape(3, NBLK, 128),
        radius.reshape(NBLK, 128),
        vertices.reshape(9, TRIBLK, 128),
        vertex_speed.reshape(9, TRIBLK, 128),
        mig_order.reshape(STEPS, NBLK, 128),
        angles,
        ghost_blocks.reshape(-1),
        tile_home.reshape(-1),
        tile_other.reshape(-1),
        wall_home.reshape(-1),
        wall_block.reshape(-1),
        mig_count.reshape(STEPS, 1, GROUP),
    )
    return (
        out[0].reshape(position.shape),
        out[1].reshape(velocity.shape),
        out[2].reshape(radius.shape),
    )


def solution(mesh):
    block = P("gx", "gy", "gz", None)
    blocks = P(None, "gx", "gy", "gz", None)
    in_specs = (
        blocks, blocks, block, blocks, blocks, P(), block, block, block, block, block, blocks, blocks,
    )
    return jax.shard_map(
        shards, mesh=mesh, in_specs=in_specs, out_specs=(blocks, blocks, block), check_vma=False
    )
```

```python
import functools

import jax
import jax.numpy as jnp
from jax import lax
from jax.experimental import pallas as pl
from jax.experimental.pallas import tpu as pltpu
from jax.sharding import PartitionSpec as P

MESH = pl.DeviceIdType.MESH
F32 = jnp.float32
BF16 = jnp.bfloat16

STEPS = 3
NBLK = 32
GHOST = 16
POOL = 128
TILES = 64
TTILES = 32
TRIBLK = 16
SLABS = 16
GROUP = 16
MC = 16
SOME = 32
SOON = 8

FAR_FIRST = [
    4 * across + along for along in (2, 1, 3, 0) for across in (1, 3, 2, 0) if along or across
]

STIFFNESS = 20.0
DAMPING = 2.0
WALL_STIFF = 20.0
SOFTENING = 0.01
TIME_STEP = 0.02
GRAVITY = 1.0
AXIS_CENTRE = 2.0
AREA_FLOOR = 1.0
SPREAD_PAD = 0.25


def split3(values):
    high = values.astype(BF16)
    rest = values - high.astype(F32)
    middle = rest.astype(BF16)
    low = (rest - middle.astype(F32)).astype(BF16)
    return high, middle, low


def split2(values):
    high = values.astype(BF16)
    low = (values - high.astype(F32)).astype(BF16)
    return high, low


def split3_wide(values):
    high = values.astype(BF16).astype(F32)
    rest = values - high
    middle = rest.astype(BF16).astype(F32)
    return high, middle, rest - middle


def swapped(block, row):
    return jnp.where(row < 3, pltpu.roll(block, 5, axis=0), pltpu.roll(block, 3, axis=0))


def over_rows(values, mask):
    total = jnp.sum(jnp.where(mask, values, 0.0), axis=0, keepdims=True)
    return jnp.broadcast_to(total, (8, 128))


def by_row(row, values):
    out = values[-1]
    for i in range(len(values) - 2, -1, -1):
        out = jnp.where(row == i, values[i], out)
    return out


def stacked(groups):
    return jnp.concatenate(groups, axis=0)


def anchor_of(home, row):
    return jnp.where(row < 6, jnp.broadcast_to(home[:, 0:1], (8, 128)), 0.0)


def pair_home(home, row):
    block = home - anchor_of(home, row)
    turned = swapped(block, row)
    norm = split3_wide(over_rows(block * block, row < 3) + SOFTENING)
    drift = split3_wide(-DAMPING * over_rows(block * turned, row < 3))
    size = split3_wide(jnp.broadcast_to(block[6:7], (8, 128)))
    zero, one = jnp.zeros((8, 128), F32), jnp.ones((8, 128), F32)
    near = [jnp.where(row < 3, -2.0 * part, 0.0) for part in split3_wide(block)]
    cross = [jnp.where(row < 6, DAMPING * part, 0.0) for part in split3_wide(turned)]
    six = (row == 6).astype(F32)
    near_end = by_row(row, [one, one, one, zero, zero, norm[0], norm[1], norm[2]])
    cross_end = by_row(
        row, [zero, zero, zero, -DAMPING * one, -DAMPING * one, drift[0], drift[1], drift[2]]
    )
    size_end = by_row(row, [zero, zero, zero, zero, zero, size[0], size[1], size[2]])
    return jnp.concatenate(
        [
            stacked([near[0], near[1], near[0], near[1], near[2], near[0], near_end, zero]),
            stacked([cross[0], cross[1], cross[0], cross[1], cross[2], cross[0], cross_end, zero]),
            stacked([six, zero, six, zero, zero, six, size_end, zero]),
        ],
        axis=1,
    ).astype(BF16)


def low_below(weights, row):
    high = weights.astype(BF16).astype(F32)
    return jnp.where(row < 4, high, pltpu.roll(weights - high, 4, axis=0)).astype(BF16)


def pair_other(other, home, row):
    block = other - anchor_of(home, row)
    turned = swapped(block, row)
    norm = split3_wide(over_rows(block * block, row < 3))
    drift = over_rows(block * turned, row < 3)
    drift_high = drift.astype(BF16).astype(F32)
    one = jnp.ones((8, 128), F32)
    end = by_row(row, [norm[0], norm[1], norm[2], drift_high, drift - drift_high, one, one, one])
    part = split3_wide(block)
    left = stacked(
        [part[0], part[0], part[1], part[1], part[0], part[2], end, jnp.zeros((8, 128), F32)]
    ).astype(BF16)
    weights = jnp.where(row < 3, block, 1.0) * jnp.broadcast_to(block[6:7], (8, 128))
    return left, low_below(weights, row)


def wall_home(home, row):
    block = home - AXIS_CENTRE
    norm = split3_wide(-over_rows(block * block, row < 3))
    parts = split3_wide(block)
    zero = jnp.zeros((8, 128), F32)
    high = [jnp.where(row < 3, part, 0.0) for part in parts]
    wide = [
        jnp.where(jnp.logical_and(row >= 3, row < 6), 2.0 * pltpu.roll(part, 3, axis=0), 0.0)
        for part in parts
    ]
    level = jnp.where(row == 7, -1.0, 0.0)
    six = (row == 6).astype(F32)
    end = by_row(row, [norm[0], norm[1], norm[2], zero])
    return jnp.concatenate(
        [
            stacked([high[0] + level, high[1], high[0] + level, high[1], high[2], high[0] + level, zero, zero]),
            stacked([wide[0] + six, wide[1], wide[0] + six, wide[1], wide[2], wide[0] + six, end, zero]),
        ],
        axis=1,
    ).astype(BF16)


def wall_other(blades, row):
    part = split3_wide(blades)
    end = jnp.where(row < 3, 1.0, 0.0)
    left = stacked(
        [part[0], part[0], part[1], part[1], part[0], part[2], end, jnp.zeros((8, 128), F32)]
    ).astype(BF16)
    reach = over_rows(blades * blades, jnp.logical_and(row >= 3, row < 6))
    weights = blades / (reach + jnp.broadcast_to(blades[6:7], (8, 128)))
    return left, low_below(weights, row)


def weighted(weights, strength):
    high, low = split2(strength)
    return jnp.dot(
        jnp.concatenate([weights, weights], axis=1),
        jnp.concatenate([high, low], axis=0),
        preferred_element_type=F32,
    )


def kernel(
    pos_h, vel_h, rad_h, vert_h, speed_h, order_h, angles, ghost_ids, home_ids, other_ids,
    wall_ids, wall_picks, counts,
    pos_o, vel_o, rad_o,
    bodies, corners, speeds, order, own, pool_0, pool_1, pool_2, lent, tri_0, tri_1, tri_2,
    outgoing, arrived, lane_hot, block_hot,
    pair_sel, wall_sel, pair_out, wall_out,
    pair_right, wall_right, wall_left, wall_weight,
    in_sem, ghost_send, ghost_recv, mig_send, mig_recv,
    zh_send, zh_recv, x_send, x_recv, xz_send, xz_recv, core_send, core_recv,
):
    pool, tri = (pool_0, pool_1, pool_2), (tri_0, tri_1, tri_2)
    gx = lax.axis_index("gx")
    gy = lax.axis_index("gy")
    gz = lax.axis_index("gz")
    me = gy * 4 + gz
    x_at, zh, core = gx // 4, (gx // 2) % 2, gx % 2
    twin = gx + 1 - 2 * core
    zmate = gx + 2 - 4 * zh

    loads = [
        pltpu.make_async_copy(vert_h, corners, in_sem.at[0]),
        pltpu.make_async_copy(speed_h, speeds, in_sem.at[1]),
        pltpu.make_async_copy(pos_h, bodies.at[pl.ds(0, 3)], in_sem.at[2]),
        pltpu.make_async_copy(vel_h, bodies.at[pl.ds(3, 3)], in_sem.at[3]),
        pltpu.make_async_copy(rad_h, bodies.at[6], in_sem.at[4]),
        pltpu.make_async_copy(order_h.at[:, pl.ds(0, 8), :], order, in_sem.at[5]),
    ]
    for load in loads:
        load.start()

    def peer_of(hop):
        row, column = lax.rem(gy + hop // 4, 4), lax.rem(gz + hop % 4, 4)
        return row * 4 + column, (gx, row, column)

    def x_mate(hop, z_of):
        index = lax.rem(x_at + hop, 4) * 4 + z_of * 2 + core
        return index

    faces = [
        (gx > 0, gx < SLABS - 1, (gx + 1, gy, gz)),
        (gx < SLABS - 1, gx > 0, (gx - 1, gy, gz)),
        (gy > 0, gy < 3, (gx, gy + 1, gz)),
        (gy < 3, gy > 0, (gx, gy - 1, gz)),
        (gz > 0, gz < 3, (gx, gy, gz + 1)),
        (gz < 3, gz > 0, (gx, gy, gz - 1)),
    ]

    barrier = pltpu.get_barrier_semaphore()

    for _, borrower, target in faces[:2]:
        @pl.when(borrower)
        def _():
            pl.semaphore_signal(barrier, inc=1, device_id=target, device_id_type=MESH)
    pl.semaphore_signal(barrier, inc=1, device_id=(zmate, gy, gz), device_id_type=MESH)
    for hop in FAR_FIRST:
        pl.semaphore_signal(barrier, inc=1, device_id=peer_of(hop)[1], device_id_type=MESH)
    for other in (x_mate(2, zh), x_mate(1, zh), x_mate(3, zh), twin):
        pl.semaphore_signal(barrier, inc=1, device_id=(other, gy, gz), device_id_type=MESH)

    def ghost_copy(step, face, target):
        return pltpu.make_async_remote_copy(
            src_ref=lent.at[step],
            dst_ref=pool[step].at[pl.ds(NBLK + GHOST * face, GHOST)],
            send_sem=ghost_send.at[step, face],
            recv_sem=ghost_recv.at[step, face],
            device_id=target,
            device_id_type=MESH,
        )

    def tri_copy(step, owner, target, send, recv):
        part = tri[step].at[pl.ds(owner * TRIBLK, TRIBLK)]
        return pltpu.make_async_remote_copy(
            src_ref=part,
            dst_ref=part,
            send_sem=send,
            recv_sem=recv,
            device_id=(target, gy, gz),
            device_id_type=MESH,
        )

    def zh_copy(step):
        return tri_copy(step, gx, zmate, zh_send.at[step], zh_recv.at[step])

    def core_copy(step, owner, slot):
        return tri_copy(step, owner, twin, core_send.at[step, slot], core_recv.at[step, slot])

    def x_copy(step, hop):
        return tri_copy(step, gx, x_mate(hop, zh), x_send.at[step, hop - 1], x_recv.at[step, hop - 1])

    def xz_copy(step, hop):
        return tri_copy(step, zmate, x_mate(hop, zh), xz_send.at[step, hop - 1], xz_recv.at[step, hop - 1])

    def mig_copy(step, hop):
        peer, target = peer_of(hop)
        return pltpu.make_async_remote_copy(
            src_ref=outgoing.at[step, peer // 8],
            dst_ref=arrived.at[step, me],
            send_sem=mig_send.at[step, hop],
            recv_sem=mig_recv.at[step, hop],
            device_id=target,
            device_id_type=MESH,
        )

    def lend(step):
        for row in range(7):
            own[:, row, :] = bodies[row]
        own[:, 7, :] = jnp.zeros((NBLK, 128), F32)
        for slot in range(GHOST):
            lent[step, slot] = own[ghost_ids[slot]]

    def send_ghosts(step):
        for face, (_, borrower, target) in enumerate(faces):
            @pl.when(borrower)
            def _():
                ghost_copy(step, face, target).start()
        pool[step][pl.ds(0, NBLK)] = own[...]

    def wait_ghosts(step):
        for face, (lender, _, target) in enumerate(faces):
            @pl.when(lender)
            def _():
                ghost_copy(step, face, target).wait_recv()

    def blade_move(step):
        angle = jnp.full((8, 128), angles[step], F32)
        cosine = jnp.cos(angle)[0:1]
        sine = jnp.sin(angle)[0:1]
        now = []
        for corner in range(3):
            along = corners[3 * corner]
            rel_y = corners[3 * corner + 1] - AXIS_CENTRE
            rel_z = corners[3 * corner + 2] - AXIS_CENTRE
            for j, value in enumerate((
                along,
                AXIS_CENTRE + cosine * rel_y - sine * rel_z,
                AXIS_CENTRE + sine * rel_y + cosine * rel_z,
            )):
                moved = value + TIME_STEP * speeds[3 * corner + j]
                corners[3 * corner + j] = moved
                now.append(moved)
        a, b, c = now[0:3], now[3:6], now[6:9]
        centre = [(a[i] + b[i] + c[i]) / 3.0 for i in range(3)]
        u = [b[i] - a[i] for i in range(3)]
        w = [c[i] - a[i] for i in range(3)]
        area = [
            u[1] * w[2] - u[2] * w[1],
            u[2] * w[0] - u[0] * w[2],
            u[0] * w[1] - u[1] * w[0],
        ]
        length = jnp.sqrt(area[0] * area[0] + area[1] * area[1] + area[2] * area[2])
        scale = 1.0 / jnp.maximum(length, AREA_FLOOR)
        normal = [area[i] * scale for i in range(3)]
        spread = SPREAD_PAD
        for corner in (a, b, c):
            for i in range(3):
                spread = spread + (corner[i] - centre[i]) ** 2 * (1.0 / 3.0)
        shifted = [centre[i] - AXIS_CENTRE for i in range(3)]
        square = shifted[0] ** 2 + shifted[1] ** 2 + shifted[2] ** 2
        level = normal[0] * shifted[0] + normal[1] * shifted[1] + normal[2] * shifted[2]
        rows = normal + shifted + [spread - square, level]
        for row in range(8):
            tri[step][pl.ds(gx * TRIBLK, TRIBLK), row, :] = rows[row]

    def start_tri(step):
        core_copy(step, gx, 0).start()
        for hop in (1, 2, 3):
            x_copy(step, hop).start()

    def forward_tri(step):
        zh_copy(step).wait_recv()
        for hop in (1, 2, 3):
            xz_copy(step, hop).start()
        core_copy(step, zmate, 1).start()

    def pass_near(step):
        for hop in (1, 2, 3):
            x_copy(step, hop).wait_recv()
            core_copy(step, x_mate(4 - hop, zh), 1 + hop).start()

    def pass_far(step):
        for hop in (1, 2, 3):
            xz_copy(step, hop).wait_recv()
            core_copy(step, x_mate(4 - hop, 1 - zh), 4 + hop).start()

    def wait_tri(step):
        for slot in range(8):
            core_copy(step, gx, slot).wait_recv()

    def prepare():
        lane = lax.broadcasted_iota(jnp.int32, (128, 256), 0)
        block = lax.broadcasted_iota(jnp.int32, (NBLK, 256), 0)
        place = lax.broadcasted_iota(jnp.int32, (1, 256), 1)
        for step in range(STEPS):
            ids = jnp.concatenate([order[step, 0:1, :], order[step, 1:2, :]], axis=1)
            lane_hot[step] = (jnp.bitwise_and(ids, 127) == lane).astype(F32).astype(BF16)
            limit = jnp.zeros((1, 256), jnp.int32)
            for peer in range(GROUP):
                limit = jnp.where(lax.shift_right_logical(place, 4) == peer, counts[step, 0, peer], limit)
            filled = jnp.bitwise_and(place, 15) < limit
            hot = lax.shift_right_logical(ids, 7) == block
            block_hot[step, 0] = hot.astype(F32)
            block_hot[step, 1] = jnp.logical_and(hot, filled).astype(F32)
        home = lax.broadcasted_iota(jnp.int32, (1, 128), 1)
        hot = [(home == home_ids[tile]).astype(F32) for tile in range(TILES)]
        pair_sel[...] = stacked(hot).T[0:NBLK].astype(BF16)
        hot = [(home == wall_ids[tile]).astype(F32) for tile in range(TTILES)]
        wall_sel[...] = stacked(hot).T[0:NBLK].astype(BF16)

    def pair_homes():
        def some(turn, carry):
            row = lax.broadcasted_iota(jnp.int32, (8, 128), 0)
            for spot in range(SOME):
                tile = turn * SOME + spot
                pair_right[tile] = pair_home(own[home_ids[tile]], row)
            return carry

        lax.fori_loop(0, TILES // SOME, some, 0)

    def pair_forces(step, halfway=None):
        row = lax.broadcasted_iota(jnp.int32, (8, 128), 0)
        ready, formed = {}, {}
        for turn in range(TILES + 2 * SOON):
            if halfway is not None and turn == TILES // 2 + SOON:
                halfway()
            if turn < TILES:
                left, weights = pair_other(
                    pool[step][other_ids[turn]], own[home_ids[turn]], row
                )
                ready[turn] = (left.T, weights)
            tile = turn - SOON
            if 0 <= tile < TILES:
                formed[tile] = jnp.dot(
                    ready[tile][0], pair_right[tile], preferred_element_type=F32
                )
            tile = turn - 2 * SOON
            if tile >= 0:
                form = formed.pop(tile)
                square = jnp.maximum(form[:, 0:128], SOFTENING)
                speed, reach = form[:, 128:256], form[:, 256:384]
                scaled = square * reach
                ratio = lax.rsqrt(scaled * reach)
                overlap = jnp.maximum(reach - scaled * ratio, 0.0)
                strength = overlap * ratio * (STIFFNESS + speed * (reach * ratio))
                pair_out[tile] = weighted(ready.pop(tile)[1], strength)

    def wall_homes():
        def some(turn, carry):
            row = lax.broadcasted_iota(jnp.int32, (8, 128), 0)
            for spot in range(SOME):
                tile = turn * SOME + spot
                wall_right[tile] = wall_home(own[wall_ids[tile]], row)
            return carry

        lax.fori_loop(0, TTILES // SOME, some, 0)

    def wall_features(step):
        def features(turn, carry):
            row = lax.broadcasted_iota(jnp.int32, (8, 128), 0)
            for spot in range(SOME):
                tile = turn * SOME + spot
                left, weights = wall_other(tri[step][wall_picks[tile]], row)
                wall_left[tile] = left.T
                wall_weight[tile] = weights
            return carry

        lax.fori_loop(0, TTILES // SOME, features, 0)

    def wall_forces():
        def forces(turn, carry):
            tiles = [turn * SOME + spot for spot in range(SOME)]
            forms = [
                jnp.dot(wall_left[tile], wall_right[tile], preferred_element_type=F32)
                for tile in tiles
            ]
            strengths = []
            for tile, form in zip(tiles, forms):
                radius = own[wall_ids[tile]][6:7, :]
                height, window = form[:, 0:128], form[:, 128:256]
                depth = jnp.maximum(radius - jnp.abs(height), 0.0)
                strengths.append(depth * height * jnp.maximum(window, 0.0))
            for tile, strength in zip(tiles, strengths):
                wall_out[tile] = weighted(wall_weight[tile], strength)
            return carry

        lax.fori_loop(0, TTILES // SOME, forces, 0)

    def integrate():
        def home_sums(select, out, rows):
            terms = [out[:, row, :] + out[:, row + 4, :] for row in range(rows)]
            parts = jnp.concatenate(split2(jnp.concatenate(terms, axis=1)), axis=0)
            both = jnp.concatenate([select, select], axis=1)
            sums = jnp.dot(both, parts, preferred_element_type=F32)
            return [sums[:, 128 * row : 128 * row + 128] for row in range(rows)]

        pairs = home_sums(pair_sel[...], pair_out, 4)
        walls = home_sums(wall_sel[...], wall_out, 3)
        weight = pairs[3]
        radius = bodies[6]
        inertia = 1.0 / (radius * radius)
        for i in range(3):
            place = bodies[i]
            contact = (place - place[:, 0:1]) * weight - pairs[i]
            pull = (contact + WALL_STIFF * walls[i]) * inertia
            if i == 2:
                pull = pull - GRAVITY
            velocity = bodies[3 + i] + TIME_STEP * pull
            bodies[3 + i] = velocity
            bodies[i] = place + TIME_STEP * velocity

    def send_migrants(step):
        hot = lane_hot[step]
        parts = stacked(split3(bodies[...].reshape(7 * NBLK, 128)))
        picked = jnp.dot(parts, hot, preferred_element_type=F32)
        picked = (picked[0:224] + picked[224:448]) + picked[448:672]
        hit = block_hot[step, 0] > 0.5
        for row in range(7):
            line = jnp.where(hit, picked[NBLK * row : NBLK * row + NBLK], 0.0)
            line = jnp.sum(line, axis=0, keepdims=True)
            outgoing[step, 0, row : row + 1, :] = line[:, 0:128]
            outgoing[step, 1, row : row + 1, :] = line[:, 128:256]
        for half in range(2):
            outgoing[step, half, 7:8, :] = jnp.zeros((1, 128), F32)

        for hop in FAR_FIRST:
            mig_copy(step, hop).start()

    def take_migrants(step):
        def wait(hop, carry):
            mig_copy(step, hop).wait_recv()
            return carry

        lax.fori_loop(1, GROUP, wait, 0)
        place = lax.shift_right_logical(lax.broadcasted_iota(jnp.int32, (8, 128), 1), 4)
        shift = (me % 8) * 16
        halves = []
        for half in range(2):
            whole = jnp.zeros((8, 128), F32)
            for spot in range(8):
                turned = pltpu.roll(
                    arrived[step, 8 * half + spot], lax.rem(16 * spot + 128 - shift, 128), axis=1
                )
                whole = jnp.where(place == spot, turned, whole)
            halves.append(whole)
        values = jnp.concatenate(halves, axis=1)
        filled = block_hot[step, 1] > 0.5
        spread = jnp.concatenate(
            [jnp.where(filled, values[row : row + 1, :], 0.0) for row in range(7)], axis=0
        )
        dims = (((1,), (1,)), ((), ()))
        hot = lane_hot[step]
        parts = stacked([*split3(spread), block_hot[step, 1].astype(BF16)])
        landed = lax.dot_general(parts, hot, dims, preferred_element_type=F32)
        hits = landed[672:704]
        landed = (landed[0:224] + landed[224:448]) + landed[448:672]
        for row in range(7):
            bodies[row] = jnp.where(hits > 0.5, landed[NBLK * row : NBLK * row + NBLK], bodies[row])

    for step in range(STEPS):
        for face, (lender, _, _) in enumerate(faces):
            @pl.when(jnp.logical_not(lender))
            def _():
                pool[step][pl.ds(NBLK + GHOST * face, GHOST)] = jnp.zeros((GHOST, 8, 128), F32)
        arrived[step, me] = jnp.zeros((8, 128), F32)

    for load in loads:
        load.wait()
    lend(0)
    blade_move(0)
    neighbours = 20 + (gx > 0).astype(jnp.int32) + (gx < SLABS - 1).astype(jnp.int32)
    pl.semaphore_wait(barrier, neighbours)

    for step in range(STEPS):
        if step == 0:
            zh_copy(0).start()
        else:
            lend(step)
        send_ghosts(step)
        if step == 0:
            start_tri(0)
            pair_homes()
            blade_move(1)
            pass_near(0)
            forward_tri(0)
            blade_move(2)
            wall_homes()
            prepare()
            wait_ghosts(0)

            def halfway():
                pass_far(0)
                zh_copy(1).start()
                start_tri(1)

            pair_forces(0, halfway)
            wait_tri(0)
            wall_features(0)
            wall_forces()
        else:
            wall_homes()
            pair_homes()
            pass_far(step)
            wait_tri(step)
            wall_features(step)
            wall_forces()
            wait_ghosts(step)
            if step == 1:
                zh_copy(2).start()
                start_tri(2)
            pair_forces(step)
        integrate()
        send_migrants(step)
        if step < 2:
            pass_near(step + 1)
            forward_tri(step + 1)
        take_migrants(step)

    pos_o[...] = bodies[0:3]
    vel_o[...] = bodies[3:6]
    rad_o[...] = bodies[6]
    for step in range(STEPS):
        for face, (_, borrower, target) in enumerate(faces):
            @pl.when(borrower)
            def _():
                ghost_copy(step, face, target).wait_send()
        zh_copy(step).wait_send()
        for hop in (1, 2, 3):
            x_copy(step, hop).wait_send()
            xz_copy(step, hop).wait_send()
        for slot in range(8):
            core_copy(step, gx, slot).wait_send()

        def wait(hop, carry):
            mig_copy(step, hop).wait_send()
            return carry

        lax.fori_loop(1, GROUP, wait, 0)


def shards(
    position, velocity, radius, vertices, vertex_speed, angles, ghost_blocks,
    tile_home, tile_other, wall_home, wall_block, mig_order, mig_count,
):
    whole = pl.BlockSpec(memory_space=pl.ANY)
    scalars = pl.BlockSpec(memory_space=pltpu.SMEM)
    here = pl.BlockSpec(memory_space=pltpu.VMEM)
    dma = pltpu.SemaphoreType.DMA
    out = pl.pallas_call(
        kernel,
        out_shape=(
            pltpu.VMEM((3, NBLK, 128), F32),
            pltpu.VMEM((3, NBLK, 128), F32),
            pltpu.VMEM((NBLK, 128), F32),
        ),
        in_specs=[whole] * 6 + [scalars] * 7,
        out_specs=(here, here, here),
        scratch_shapes=[
            pltpu.VMEM((7, NBLK, 128), F32),
            pltpu.VMEM((9, TRIBLK, 128), F32),
            pltpu.VMEM((9, TRIBLK, 128), F32),
            pltpu.VMEM((STEPS, 8, 128), jnp.int32),
            pltpu.VMEM((NBLK, 8, 128), F32),
            *[pltpu.VMEM((POOL, 8, 128), F32) for _ in range(STEPS)],
            pltpu.VMEM((STEPS, GHOST, 8, 128), F32),
            *[pltpu.VMEM((SLABS * TRIBLK, 8, 128), F32) for _ in range(STEPS)],
            pltpu.VMEM((STEPS, 2, 8, 128), F32),
            pltpu.VMEM((STEPS, GROUP, 8, 128), F32),
            pltpu.VMEM((STEPS, 128, 256), BF16),
            pltpu.VMEM((STEPS, 2, NBLK, 256), F32),
            pltpu.VMEM((NBLK, TILES), BF16),
            pltpu.VMEM((NBLK, TTILES), BF16),
            pltpu.VMEM((TILES, 8, 128), F32),
            pltpu.VMEM((TTILES, 8, 128), F32),
            pltpu.VMEM((TILES, 64, 384), BF16),
            pltpu.VMEM((TTILES, 64, 256), BF16),
            pltpu.VMEM((TTILES, 128, 64), BF16),
            pltpu.VMEM((TTILES, 8, 128), BF16),
            dma((6,)),
            dma((STEPS, 6)),
            dma((STEPS, 6)),
            dma((STEPS, GROUP)),
            dma((STEPS, GROUP)),
            dma((STEPS,)),
            dma((STEPS,)),
            dma((STEPS, 3)),
            dma((STEPS, 3)),
            dma((STEPS, 3)),
            dma((STEPS, 3)),
            dma((STEPS, 8)),
            dma((STEPS, 8)),
        ],
        compiler_params=pltpu.CompilerParams(
            collective_id=0, has_side_effects=True, vmem_limit_bytes=60 * 1024 * 1024
        ),
    )(
        position.reshape(3, NBLK, 128),
        velocity.reshape(3, NBLK, 128),
        radius.reshape(NBLK, 128),
        vertices.reshape(9, TRIBLK, 128),
        vertex_speed.reshape(9, TRIBLK, 128),
        mig_order.reshape(STEPS, NBLK, 128),
        angles,
        ghost_blocks.reshape(-1),
        tile_home.reshape(-1),
        tile_other.reshape(-1),
        wall_home.reshape(-1),
        wall_block.reshape(-1),
        mig_count.reshape(STEPS, 1, GROUP),
    )
    return (
        out[0].reshape(position.shape),
        out[1].reshape(velocity.shape),
        out[2].reshape(radius.shape),
    )


def solution(mesh):
    block = P("gx", "gy", "gz", None)
    blocks = P(None, "gx", "gy", "gz", None)
    in_specs = (
        blocks, blocks, block, blocks, blocks, P(), block, block, block, block, block, blocks, blocks,
    )
    return jax.shard_map(
        shards, mesh=mesh, in_specs=in_specs, out_specs=(blocks, blocks, block), check_vma=False
    )
```

```python
import functools

import jax
import jax.numpy as jnp
from jax import lax
from jax.experimental import pallas as pl
from jax.experimental.pallas import tpu as pltpu
from jax.sharding import PartitionSpec as P

MESH = pl.DeviceIdType.MESH
F32 = jnp.float32
BF16 = jnp.bfloat16

STEPS = 3
NBLK = 32
GHOST = 16
POOL = 128
TILES = 64
TTILES = 32
TRIBLK = 16
HALF = 8
SLABS = 16
GROUP = 16
MC = 16
SOME = 32
SOON = 8

FAR_FIRST = [
    4 * across + along for along in (2, 1, 3, 0) for across in (1, 3, 2, 0) if along or across
]

STIFFNESS = 20.0
DAMPING = 2.0
WALL_STIFF = 20.0
SOFTENING = 0.01
TIME_STEP = 0.02
GRAVITY = 1.0
AXIS_CENTRE = 2.0
AREA_FLOOR = 1.0
SPREAD_PAD = 0.25


def split3(values):
    high = values.astype(BF16)
    rest = values - high.astype(F32)
    middle = rest.astype(BF16)
    low = (rest - middle.astype(F32)).astype(BF16)
    return high, middle, low


def split2(values):
    high = values.astype(BF16)
    low = (values - high.astype(F32)).astype(BF16)
    return high, low


def split3_wide(values):
    high = values.astype(BF16).astype(F32)
    rest = values - high
    middle = rest.astype(BF16).astype(F32)
    return high, middle, rest - middle


def swapped(block, row):
    return jnp.where(row < 3, pltpu.roll(block, 5, axis=0), pltpu.roll(block, 3, axis=0))


def over_rows(values, mask):
    total = jnp.sum(jnp.where(mask, values, 0.0), axis=0, keepdims=True)
    return jnp.broadcast_to(total, (8, 128))


def by_row(row, values):
    out = values[-1]
    for i in range(len(values) - 2, -1, -1):
        out = jnp.where(row == i, values[i], out)
    return out


def stacked(groups):
    return jnp.concatenate(groups, axis=0)


def anchor_of(home, row):
    return jnp.where(row < 6, jnp.broadcast_to(home[:, 0:1], (8, 128)), 0.0)


def pair_home(home, row):
    block = home - anchor_of(home, row)
    turned = swapped(block, row)
    norm = split3_wide(over_rows(block * block, row < 3) + SOFTENING)
    drift = split3_wide(-DAMPING * over_rows(block * turned, row < 3))
    size = split3_wide(jnp.broadcast_to(block[6:7], (8, 128)))
    zero, one = jnp.zeros((8, 128), F32), jnp.ones((8, 128), F32)
    near = [jnp.where(row < 3, -2.0 * part, 0.0) for part in split3_wide(block)]
    cross = [jnp.where(row < 6, DAMPING * part, 0.0) for part in split3_wide(turned)]
    six = (row == 6).astype(F32)
    near_end = by_row(row, [one, one, one, zero, zero, norm[0], norm[1], norm[2]])
    cross_end = by_row(
        row, [zero, zero, zero, -DAMPING * one, -DAMPING * one, drift[0], drift[1], drift[2]]
    )
    size_end = by_row(row, [zero, zero, zero, zero, zero, size[0], size[1], size[2]])
    return jnp.concatenate(
        [
            stacked([near[0], near[1], near[0], near[1], near[2], near[0], near_end, zero]),
            stacked([cross[0], cross[1], cross[0], cross[1], cross[2], cross[0], cross_end, zero]),
            stacked([six, zero, six, zero, zero, six, size_end, zero]),
        ],
        axis=1,
    ).astype(BF16)


def low_below(weights, row):
    high = weights.astype(BF16).astype(F32)
    return jnp.where(row < 4, high, pltpu.roll(weights - high, 4, axis=0)).astype(BF16)


def pair_other(other, home, row):
    block = other - anchor_of(home, row)
    turned = swapped(block, row)
    norm = split3_wide(over_rows(block * block, row < 3))
    drift = over_rows(block * turned, row < 3)
    drift_high = drift.astype(BF16).astype(F32)
    one = jnp.ones((8, 128), F32)
    end = by_row(row, [norm[0], norm[1], norm[2], drift_high, drift - drift_high, one, one, one])
    part = split3_wide(block)
    left = stacked(
        [part[0], part[0], part[1], part[1], part[0], part[2], end, jnp.zeros((8, 128), F32)]
    ).astype(BF16)
    weights = jnp.where(row < 3, block, 1.0) * jnp.broadcast_to(block[6:7], (8, 128))
    return left, low_below(weights, row)


def wall_home(home, row):
    block = home - AXIS_CENTRE
    norm = split3_wide(-over_rows(block * block, row < 3))
    parts = split3_wide(block)
    zero = jnp.zeros((8, 128), F32)
    high = [jnp.where(row < 3, part, 0.0) for part in parts]
    wide = [
        jnp.where(jnp.logical_and(row >= 3, row < 6), 2.0 * pltpu.roll(part, 3, axis=0), 0.0)
        for part in parts
    ]
    level = jnp.where(row == 7, -1.0, 0.0)
    six = (row == 6).astype(F32)
    end = by_row(row, [norm[0], norm[1], norm[2], zero])
    return jnp.concatenate(
        [
            stacked([high[0] + level, high[1], high[0] + level, high[1], high[2], high[0] + level, zero, zero]),
            stacked([wide[0] + six, wide[1], wide[0] + six, wide[1], wide[2], wide[0] + six, end, zero]),
        ],
        axis=1,
    ).astype(BF16)


def wall_other(blades, row):
    part = split3_wide(blades)
    end = jnp.where(row < 3, 1.0, 0.0)
    left = stacked(
        [part[0], part[0], part[1], part[1], part[0], part[2], end, jnp.zeros((8, 128), F32)]
    ).astype(BF16)
    reach = over_rows(blades * blades, jnp.logical_and(row >= 3, row < 6))
    weights = blades / (reach + jnp.broadcast_to(blades[6:7], (8, 128)))
    return left, low_below(weights, row)


def weighted(weights, strength):
    high, low = split2(strength)
    return jnp.dot(
        jnp.concatenate([weights, weights], axis=1),
        jnp.concatenate([high, low], axis=0),
        preferred_element_type=F32,
    )


def kernel(
    pos_h, vel_h, rad_h, vert_h, speed_h, order_h, angles, ghost_ids, home_ids, other_ids,
    wall_ids, wall_picks, counts,
    pos_o, vel_o, rad_o,
    bodies, corners, speeds, order, own, pool_0, pool_1, pool_2, lent, tri_0, tri_1, tri_2,
    outgoing, arrived, lane_hot, block_hot,
    pair_sel, wall_sel, pair_out, wall_out,
    pair_right, wall_right, wall_left, wall_weight,
    in_sem, ghost_send, ghost_recv, mig_send, mig_recv,
    zh_send, zh_recv, x_send, x_recv, xz_send, xz_recv, core_send, core_recv,
):
    pool, tri = (pool_0, pool_1, pool_2), (tri_0, tri_1, tri_2)
    gx = lax.axis_index("gx")
    gy = lax.axis_index("gy")
    gz = lax.axis_index("gz")
    me = gy * 4 + gz
    x_at, zh, core = gx // 4, (gx // 2) % 2, gx % 2
    twin = gx + 1 - 2 * core
    zmate = gx + 2 - 4 * zh

    loads = [
        pltpu.make_async_copy(vert_h, corners, in_sem.at[0]),
        pltpu.make_async_copy(speed_h, speeds, in_sem.at[1]),
        pltpu.make_async_copy(pos_h, bodies.at[pl.ds(0, 3)], in_sem.at[2]),
        pltpu.make_async_copy(vel_h, bodies.at[pl.ds(3, 3)], in_sem.at[3]),
        pltpu.make_async_copy(rad_h, bodies.at[6], in_sem.at[4]),
        pltpu.make_async_copy(order_h.at[:, pl.ds(0, 8), :], order, in_sem.at[5]),
    ]
    for load in loads:
        load.start()

    def peer_of(hop):
        row, column = lax.rem(gy + hop // 4, 4), lax.rem(gz + hop % 4, 4)
        return row * 4 + column, (gx, row, column)

    def x_mate(hop, z_of):
        index = lax.rem(x_at + hop, 4) * 4 + z_of * 2 + core
        return index

    faces = [
        (gx > 0, gx < SLABS - 1, (gx + 1, gy, gz)),
        (gx < SLABS - 1, gx > 0, (gx - 1, gy, gz)),
        (gy > 0, gy < 3, (gx, gy + 1, gz)),
        (gy < 3, gy > 0, (gx, gy - 1, gz)),
        (gz > 0, gz < 3, (gx, gy, gz + 1)),
        (gz < 3, gz > 0, (gx, gy, gz - 1)),
    ]

    barrier = pltpu.get_barrier_semaphore()

    for _, borrower, target in faces[:2]:
        @pl.when(borrower)
        def _():
            pl.semaphore_signal(barrier, inc=1, device_id=target, device_id_type=MESH)
    pl.semaphore_signal(barrier, inc=1, device_id=(zmate, gy, gz), device_id_type=MESH)
    for hop in FAR_FIRST:
        pl.semaphore_signal(barrier, inc=1, device_id=peer_of(hop)[1], device_id_type=MESH)
    for other in (x_mate(2, zh), x_mate(1, zh), x_mate(3, zh), twin):
        pl.semaphore_signal(barrier, inc=1, device_id=(other, gy, gz), device_id_type=MESH)

    def ghost_copy(step, face, target):
        return pltpu.make_async_remote_copy(
            src_ref=lent.at[step],
            dst_ref=pool[step].at[pl.ds(NBLK + GHOST * face, GHOST)],
            send_sem=ghost_send.at[step, face],
            recv_sem=ghost_recv.at[step, face],
            device_id=target,
            device_id_type=MESH,
        )

    def tri_copy(step, owner, target, send, recv, first=0, count=TRIBLK):
        part = tri[step].at[pl.ds(owner * TRIBLK + first, count)]
        return pltpu.make_async_remote_copy(
            src_ref=part,
            dst_ref=part,
            send_sem=send,
            recv_sem=recv,
            device_id=(target, gy, gz),
            device_id_type=MESH,
        )

    def zh_copy(step, half):
        return tri_copy(
            step, gx, zmate, zh_send.at[step, half], zh_recv.at[step, half], HALF * half, HALF
        )

    def start_zh(step):
        for half in range(2):
            zh_copy(step, half).start()

    def core_copy(step, owner, slot):
        return tri_copy(step, owner, twin, core_send.at[step, slot], core_recv.at[step, slot])

    def x_copy(step, hop):
        return tri_copy(step, gx, x_mate(hop, zh), x_send.at[step, hop - 1], x_recv.at[step, hop - 1])

    def xz_copy(step, hop, half):
        slot = 2 * (hop - 1) + half
        return tri_copy(
            step, zmate, x_mate(hop, zh), xz_send.at[step, slot], xz_recv.at[step, slot],
            HALF * half, HALF,
        )

    def mig_copy(step, hop):
        peer, target = peer_of(hop)
        return pltpu.make_async_remote_copy(
            src_ref=outgoing.at[step, peer // 8],
            dst_ref=arrived.at[step, me],
            send_sem=mig_send.at[step, hop],
            recv_sem=mig_recv.at[step, hop],
            device_id=target,
            device_id_type=MESH,
        )

    def lend(step):
        for row in range(7):
            own[:, row, :] = bodies[row]
        own[:, 7, :] = jnp.zeros((NBLK, 128), F32)
        for slot in range(GHOST):
            lent[step, slot] = own[ghost_ids[slot]]

    def send_ghosts(step):
        for face, (_, borrower, target) in enumerate(faces):
            @pl.when(borrower)
            def _():
                ghost_copy(step, face, target).start()
        pool[step][pl.ds(0, NBLK)] = own[...]

    def wait_ghosts(step):
        for face, (lender, _, target) in enumerate(faces):
            @pl.when(lender)
            def _():
                ghost_copy(step, face, target).wait_recv()

    def blade_move(step):
        angle = jnp.full((8, 128), angles[step], F32)
        cosine = jnp.cos(angle)[0:1]
        sine = jnp.sin(angle)[0:1]
        now = []
        for corner in range(3):
            along = corners[3 * corner]
            rel_y = corners[3 * corner + 1] - AXIS_CENTRE
            rel_z = corners[3 * corner + 2] - AXIS_CENTRE
            for j, value in enumerate((
                along,
                AXIS_CENTRE + cosine * rel_y - sine * rel_z,
                AXIS_CENTRE + sine * rel_y + cosine * rel_z,
            )):
                moved = value + TIME_STEP * speeds[3 * corner + j]
                corners[3 * corner + j] = moved
                now.append(moved)
        a, b, c = now[0:3], now[3:6], now[6:9]
        centre = [(a[i] + b[i] + c[i]) / 3.0 for i in range(3)]
        u = [b[i] - a[i] for i in range(3)]
        w = [c[i] - a[i] for i in range(3)]
        area = [
            u[1] * w[2] - u[2] * w[1],
            u[2] * w[0] - u[0] * w[2],
            u[0] * w[1] - u[1] * w[0],
        ]
        length = jnp.sqrt(area[0] * area[0] + area[1] * area[1] + area[2] * area[2])
        scale = 1.0 / jnp.maximum(length, AREA_FLOOR)
        normal = [area[i] * scale for i in range(3)]
        spread = SPREAD_PAD
        for corner in (a, b, c):
            for i in range(3):
                spread = spread + (corner[i] - centre[i]) ** 2 * (1.0 / 3.0)
        shifted = [centre[i] - AXIS_CENTRE for i in range(3)]
        square = shifted[0] ** 2 + shifted[1] ** 2 + shifted[2] ** 2
        level = normal[0] * shifted[0] + normal[1] * shifted[1] + normal[2] * shifted[2]
        rows = normal + shifted + [spread - square, level]
        for row in range(8):
            tri[step][pl.ds(gx * TRIBLK, TRIBLK), row, :] = rows[row]

    def start_tri(step):
        core_copy(step, gx, 0).start()
        for hop in (1, 2, 3):
            x_copy(step, hop).start()

    def forward_tri(step):
        for half in range(2):
            zh_copy(step, half).wait_recv()
            for hop in (2, 1, 3):
                xz_copy(step, hop, half).start()
        core_copy(step, zmate, 1).start()

    def pass_near(step):
        for hop in (1, 2, 3):
            x_copy(step, hop).wait_recv()
            core_copy(step, x_mate(4 - hop, zh), 1 + hop).start()

    def pass_far(step):
        for hop in (1, 3, 2):
            for half in range(2):
                xz_copy(step, hop, half).wait_recv()
            core_copy(step, x_mate(4 - hop, 1 - zh), 4 + hop).start()

    def wait_tri(step):
        for slot in range(8):
            core_copy(step, gx, slot).wait_recv()

    def prepare():
        lane = lax.broadcasted_iota(jnp.int32, (128, 256), 0)
        block = lax.broadcasted_iota(jnp.int32, (NBLK, 256), 0)
        place = lax.broadcasted_iota(jnp.int32, (1, 256), 1)
        for step in range(STEPS):
            ids = jnp.concatenate([order[step, 0:1, :], order[step, 1:2, :]], axis=1)
            lane_hot[step] = (jnp.bitwise_and(ids, 127) == lane).astype(F32).astype(BF16)
            limit = jnp.zeros((1, 256), jnp.int32)
            for peer in range(GROUP):
                limit = jnp.where(lax.shift_right_logical(place, 4) == peer, counts[step, 0, peer], limit)
            filled = jnp.bitwise_and(place, 15) < limit
            hot = lax.shift_right_logical(ids, 7) == block
            block_hot[step, 0] = hot.astype(F32)
            block_hot[step, 1] = jnp.logical_and(hot, filled).astype(F32)
        home = lax.broadcasted_iota(jnp.int32, (1, 128), 1)
        hot = [(home == home_ids[tile]).astype(F32) for tile in range(TILES)]
        pair_sel[...] = stacked(hot).T[0:NBLK].astype(BF16)
        hot = [(home == wall_ids[tile]).astype(F32) for tile in range(TTILES)]
        wall_sel[...] = stacked(hot).T[0:NBLK].astype(BF16)

    def pair_homes():
        def some(turn, carry):
            row = lax.broadcasted_iota(jnp.int32, (8, 128), 0)
            for spot in range(SOME):
                tile = turn * SOME + spot
                pair_right[tile] = pair_home(own[home_ids[tile]], row)
            return carry

        lax.fori_loop(0, TILES // SOME, some, 0)

    def pair_forces(step, halfway=None):
        row = lax.broadcasted_iota(jnp.int32, (8, 128), 0)
        ready, formed = {}, {}
        for turn in range(TILES + 2 * SOON):
            if halfway is not None and turn == TILES // 2 + SOON:
                halfway()
            if turn < TILES:
                left, weights = pair_other(
                    pool[step][other_ids[turn]], own[home_ids[turn]], row
                )
                ready[turn] = (left.T, weights)
            tile = turn - SOON
            if 0 <= tile < TILES:
                formed[tile] = jnp.dot(
                    ready[tile][0], pair_right[tile], preferred_element_type=F32
                )
            tile = turn - 2 * SOON
            if tile >= 0:
                form = formed.pop(tile)
                square = jnp.maximum(form[:, 0:128], SOFTENING)
                speed, reach = form[:, 128:256], form[:, 256:384]
                scaled = square * reach
                ratio = lax.rsqrt(scaled * reach)
                overlap = jnp.maximum(reach - scaled * ratio, 0.0)
                strength = overlap * ratio * (STIFFNESS + speed * (reach * ratio))
                pair_out[tile] = weighted(ready.pop(tile)[1], strength)

    def wall_homes():
        def some(turn, carry):
            row = lax.broadcasted_iota(jnp.int32, (8, 128), 0)
            for spot in range(SOME):
                tile = turn * SOME + spot
                wall_right[tile] = wall_home(own[wall_ids[tile]], row)
            return carry

        lax.fori_loop(0, TTILES // SOME, some, 0)

    def wall_features(step):
        def features(turn, carry):
            row = lax.broadcasted_iota(jnp.int32, (8, 128), 0)
            for spot in range(SOME):
                tile = turn * SOME + spot
                left, weights = wall_other(tri[step][wall_picks[tile]], row)
                wall_left[tile] = left.T
                wall_weight[tile] = weights
            return carry

        lax.fori_loop(0, TTILES // SOME, features, 0)

    def wall_forces():
        def forces(turn, carry):
            tiles = [turn * SOME + spot for spot in range(SOME)]
            forms = [
                jnp.dot(wall_left[tile], wall_right[tile], preferred_element_type=F32)
                for tile in tiles
            ]
            strengths = []
            for tile, form in zip(tiles, forms):
                radius = own[wall_ids[tile]][6:7, :]
                height, window = form[:, 0:128], form[:, 128:256]
                depth = jnp.maximum(radius - jnp.abs(height), 0.0)
                strengths.append(depth * height * jnp.maximum(window, 0.0))
            for tile, strength in zip(tiles, strengths):
                wall_out[tile] = weighted(wall_weight[tile], strength)
            return carry

        lax.fori_loop(0, TTILES // SOME, forces, 0)

    def integrate():
        def home_sums(select, out, rows):
            terms = [out[:, row, :] + out[:, row + 4, :] for row in range(rows)]
            parts = jnp.concatenate(split2(jnp.concatenate(terms, axis=1)), axis=0)
            both = jnp.concatenate([select, select], axis=1)
            sums = jnp.dot(both, parts, preferred_element_type=F32)
            return [sums[:, 128 * row : 128 * row + 128] for row in range(rows)]

        pairs = home_sums(pair_sel[...], pair_out, 4)
        walls = home_sums(wall_sel[...], wall_out, 3)
        weight = pairs[3]
        radius = bodies[6]
        inertia = 1.0 / (radius * radius)
        for i in range(3):
            place = bodies[i]
            contact = (place - place[:, 0:1]) * weight - pairs[i]
            pull = (contact + WALL_STIFF * walls[i]) * inertia
            if i == 2:
                pull = pull - GRAVITY
            velocity = bodies[3 + i] + TIME_STEP * pull
            bodies[3 + i] = velocity
            bodies[i] = place + TIME_STEP * velocity

    def send_migrants(step):
        hot = lane_hot[step]
        parts = stacked(split3(bodies[...].reshape(7 * NBLK, 128)))
        picked = jnp.dot(parts, hot, preferred_element_type=F32)
        picked = (picked[0:224] + picked[224:448]) + picked[448:672]
        hit = block_hot[step, 0] > 0.5
        for row in range(7):
            line = jnp.where(hit, picked[NBLK * row : NBLK * row + NBLK], 0.0)
            line = jnp.sum(line, axis=0, keepdims=True)
            outgoing[step, 0, row : row + 1, :] = line[:, 0:128]
            outgoing[step, 1, row : row + 1, :] = line[:, 128:256]
        for half in range(2):
            outgoing[step, half, 7:8, :] = jnp.zeros((1, 128), F32)

        for hop in FAR_FIRST:
            mig_copy(step, hop).start()

    def take_migrants(step):
        def wait(hop, carry):
            mig_copy(step, hop).wait_recv()
            return carry

        lax.fori_loop(1, GROUP, wait, 0)
        place = lax.shift_right_logical(lax.broadcasted_iota(jnp.int32, (8, 128), 1), 4)
        shift = (me % 8) * 16
        halves = []
        for half in range(2):
            whole = jnp.zeros((8, 128), F32)
            for spot in range(8):
                turned = pltpu.roll(
                    arrived[step, 8 * half + spot], lax.rem(16 * spot + 128 - shift, 128), axis=1
                )
                whole = jnp.where(place == spot, turned, whole)
            halves.append(whole)
        values = jnp.concatenate(halves, axis=1)
        filled = block_hot[step, 1] > 0.5
        spread = jnp.concatenate(
            [jnp.where(filled, values[row : row + 1, :], 0.0) for row in range(7)], axis=0
        )
        dims = (((1,), (1,)), ((), ()))
        hot = lane_hot[step]
        parts = stacked([*split3(spread), block_hot[step, 1].astype(BF16)])
        landed = lax.dot_general(parts, hot, dims, preferred_element_type=F32)
        hits = landed[672:704]
        landed = (landed[0:224] + landed[224:448]) + landed[448:672]
        for row in range(7):
            bodies[row] = jnp.where(hits > 0.5, landed[NBLK * row : NBLK * row + NBLK], bodies[row])

    for step in range(STEPS):
        for face, (lender, _, _) in enumerate(faces):
            @pl.when(jnp.logical_not(lender))
            def _():
                pool[step][pl.ds(NBLK + GHOST * face, GHOST)] = jnp.zeros((GHOST, 8, 128), F32)
        arrived[step, me] = jnp.zeros((8, 128), F32)

    for load in loads:
        load.wait()
    lend(0)
    blade_move(0)
    neighbours = 20 + (gx > 0).astype(jnp.int32) + (gx < SLABS - 1).astype(jnp.int32)
    pl.semaphore_wait(barrier, neighbours)

    for step in range(STEPS):
        if step == 0:
            start_zh(0)
        else:
            lend(step)
        send_ghosts(step)
        if step == 0:
            start_tri(0)
            pair_homes()
            blade_move(1)
            pass_near(0)
            forward_tri(0)
            blade_move(2)
            wall_homes()
            prepare()
            wait_ghosts(0)

            def halfway():
                pass_far(0)
                start_zh(1)
                start_tri(1)

            pair_forces(0, halfway)
            wait_tri(0)
            wall_features(0)
            wall_forces()
        else:
            wall_homes()
            pair_homes()
            pass_far(step)
            wait_tri(step)
            wall_features(step)
            wall_forces()
            wait_ghosts(step)
            if step == 1:
                start_zh(2)
                start_tri(2)
            pair_forces(step)
        integrate()
        send_migrants(step)
        if step < 2:
            pass_near(step + 1)
            forward_tri(step + 1)
        take_migrants(step)

    pos_o[...] = bodies[0:3]
    vel_o[...] = bodies[3:6]
    rad_o[...] = bodies[6]
    for step in range(STEPS):
        for face, (_, borrower, target) in enumerate(faces):
            @pl.when(borrower)
            def _():
                ghost_copy(step, face, target).wait_send()
        for half in range(2):
            zh_copy(step, half).wait_send()
            for hop in (1, 2, 3):
                xz_copy(step, hop, half).wait_send()
        for hop in (1, 2, 3):
            x_copy(step, hop).wait_send()
        for slot in range(8):
            core_copy(step, gx, slot).wait_send()

        def wait(hop, carry):
            mig_copy(step, hop).wait_send()
            return carry

        lax.fori_loop(1, GROUP, wait, 0)


def shards(
    position, velocity, radius, vertices, vertex_speed, angles, ghost_blocks,
    tile_home, tile_other, wall_home, wall_block, mig_order, mig_count,
):
    whole = pl.BlockSpec(memory_space=pl.ANY)
    scalars = pl.BlockSpec(memory_space=pltpu.SMEM)
    here = pl.BlockSpec(memory_space=pltpu.VMEM)
    dma = pltpu.SemaphoreType.DMA
    out = pl.pallas_call(
        kernel,
        out_shape=(
            pltpu.VMEM((3, NBLK, 128), F32),
            pltpu.VMEM((3, NBLK, 128), F32),
            pltpu.VMEM((NBLK, 128), F32),
        ),
        in_specs=[whole] * 6 + [scalars] * 7,
        out_specs=(here, here, here),
        scratch_shapes=[
            pltpu.VMEM((7, NBLK, 128), F32),
            pltpu.VMEM((9, TRIBLK, 128), F32),
            pltpu.VMEM((9, TRIBLK, 128), F32),
            pltpu.VMEM((STEPS, 8, 128), jnp.int32),
            pltpu.VMEM((NBLK, 8, 128), F32),
            *[pltpu.VMEM((POOL, 8, 128), F32) for _ in range(STEPS)],
            pltpu.VMEM((STEPS, GHOST, 8, 128), F32),
            *[pltpu.VMEM((SLABS * TRIBLK, 8, 128), F32) for _ in range(STEPS)],
            pltpu.VMEM((STEPS, 2, 8, 128), F32),
            pltpu.VMEM((STEPS, GROUP, 8, 128), F32),
            pltpu.VMEM((STEPS, 128, 256), BF16),
            pltpu.VMEM((STEPS, 2, NBLK, 256), F32),
            pltpu.VMEM((NBLK, TILES), BF16),
            pltpu.VMEM((NBLK, TTILES), BF16),
            pltpu.VMEM((TILES, 8, 128), F32),
            pltpu.VMEM((TTILES, 8, 128), F32),
            pltpu.VMEM((TILES, 64, 384), BF16),
            pltpu.VMEM((TTILES, 64, 256), BF16),
            pltpu.VMEM((TTILES, 128, 64), BF16),
            pltpu.VMEM((TTILES, 8, 128), BF16),
            dma((6,)),
            dma((STEPS, 6)),
            dma((STEPS, 6)),
            dma((STEPS, GROUP)),
            dma((STEPS, GROUP)),
            dma((STEPS, 2)),
            dma((STEPS, 2)),
            dma((STEPS, 3)),
            dma((STEPS, 3)),
            dma((STEPS, 6)),
            dma((STEPS, 6)),
            dma((STEPS, 8)),
            dma((STEPS, 8)),
        ],
        compiler_params=pltpu.CompilerParams(
            collective_id=0, has_side_effects=True, vmem_limit_bytes=60 * 1024 * 1024
        ),
    )(
        position.reshape(3, NBLK, 128),
        velocity.reshape(3, NBLK, 128),
        radius.reshape(NBLK, 128),
        vertices.reshape(9, TRIBLK, 128),
        vertex_speed.reshape(9, TRIBLK, 128),
        mig_order.reshape(STEPS, NBLK, 128),
        angles,
        ghost_blocks.reshape(-1),
        tile_home.reshape(-1),
        tile_other.reshape(-1),
        wall_home.reshape(-1),
        wall_block.reshape(-1),
        mig_count.reshape(STEPS, 1, GROUP),
    )
    return (
        out[0].reshape(position.shape),
        out[1].reshape(velocity.shape),
        out[2].reshape(radius.shape),
    )


def solution(mesh):
    block = P("gx", "gy", "gz", None)
    blocks = P(None, "gx", "gy", "gz", None)
    in_specs = (
        blocks, blocks, block, blocks, blocks, P(), block, block, block, block, block, blocks, blocks,
    )
    return jax.shard_map(
        shards, mesh=mesh, in_specs=in_specs, out_specs=(blocks, blocks, block), check_vma=False
    )
```
